32 devices in a mesh: group: 2 (over y), row: 4 (over z), col: 2 (over x), sub: 2 (over core).
Axes of the slice: x: 2, y: 2, z: 4, core: 2. Of those that a mesh axis runs over, the one named last changes fastest.
Arguments:
- traces: bfloat16 [8, 5120, 16384], P(('group', 'sub'), 'col', 'row'), parts along dimension 0, may hold values from -200 to 200
- quality_mask: int32 [5120], P('col'), may hold values 0 or 1
- band_bins: int32 [128], replicated, may hold values from 17 to 163, as said below
Outputs:
- correlation: float32 [8, 5120, 5120], P('group', 'row', ('col', 'sub')), parts along dimension 0
The draws below stay inside these ranges and needn't reach their ends.
There are 2 independent parts, one for each index of `group`. The reference program is written for one: setup_inputs(seed, part) draws one part's arguments, and reference() takes and returns one part's arrays. A program takes and returns all parts, laid end to end along the dimension named above; an argument that names none is the same for every part. Nothing has to cross between parts.
Inputs may be any that keep to these rules, and one draw needn't show every extreme that they name: `band_bins`: 128 distinct bin numbers; the lowest and the highest bin of the band are among them.
All inputs are finite; a program needn't handle non-finite values. No bound on the sum of `quality_mask` on one device may be relied on, other than what follows from the above.
Results may differ from the reference program's by a relative error of at most 0.0053.
Values may be sent and summed in bfloat16 or wider, within the bound.
No kernel may reach another device: no remote copies, remote signals or barrier semaphores. Data moves between devices by JAX's collectives and lax.ppermute only.
A program may use at most 320 MiB of HBM per device.

```python
import math
import jax
import jax.numpy as jnp
from jax import lax

C = 5120
W = 16384
K = 128
LAGS = 4
LAG_STEP = 50
NWIN = 4
BLO = 17
BHI = 164
N_ROW = 4
N_COL = 2


def draw_traces(key, part):
    key = jax.random.fold_in(key, 11)
    keys = jax.random.split(key, 5)
    noise = jnp.clip(jax.random.normal(keys[0], (NWIN, C, W), jnp.float32), -6.0, 6.0)
    gains = jnp.exp(jax.random.uniform(keys[1], (1, C, 1), jnp.float32, 0.0, math.log(10.0)))
    tone_bin = jax.random.randint(keys[2], (1, C, 1), BLO, BHI)
    tone_phase = jax.random.uniform(keys[3], (1, C, 1), jnp.float32, -math.pi, math.pi)
    tone_size = jax.random.uniform(keys[4], (1, C, 1), jnp.float32, 0.02, 0.2)
    sample_times = jnp.arange(W, dtype=jnp.int32)[None, None, :]
    phase_index = tone_bin * sample_times % W
    tone = tone_size * jnp.cos(2.0 * math.pi / W * phase_index.astype(jnp.float32) + tone_phase)
    return (gains * (noise + tone)).astype(jnp.bfloat16)


def draw_band_bins(key, part):
    key = jax.random.fold_in(key, 12)
    middle = jax.random.permutation(key, BHI - BLO - 2)[:K - 2] + BLO + 1
    ends = jnp.array([BLO, BHI - 1], dtype=jnp.int32)
    return jnp.concatenate([ends, middle.astype(jnp.int32)])


def with_ends(entries, stream_key, low, high):
    longest = entries.shape.index(max(entries.shape))
    spots = []
    for shift in (0, 1):
        where = [jax.random.randint(jax.random.fold_in(stream_key, axis), (), 0, length) for axis, length in enumerate(entries.shape)]
        where[longest] = (where[longest] + shift) % entries.shape[longest]
        spots.append(tuple(where))
    return entries.at[spots[0]].set(low).at[spots[1]].set(high)


def setup_inputs(seed: int = 0, part: int = 0) -> dict:
    streams_of = jax.random.split(jax.random.key(seed), 4)
    own_keys = jax.random.split(jax.random.fold_in(streams_of[3], part), 4)
    traces = draw_traces(jax.random.fold_in(jax.random.fold_in(streams_of[3], part), 71), part)
    quality_mask = with_ends((jax.random.randint(streams_of[1], (C,), 0, 8) < 7).astype(jnp.int32), jax.random.fold_in(streams_of[1], 1), 0, 1)
    band_bins = draw_band_bins(jax.random.fold_in(streams_of[3], 71), part)
    return dict(traces=traces, quality_mask=quality_mask, band_bins=band_bins)


TWO_PI = 2.0 * math.pi

def band_table(sample_times, bin_ids, length):
    window_taper = 0.5 - 0.5 * jnp.cos(TWO_PI / length * sample_times.astype(jnp.float32))
    phase_index = sample_times[:, None] * bin_ids[None, :] % length
    angles = TWO_PI / length * phase_index.astype(jnp.float32)
    cosine = window_taper[:, None] * jnp.cos(angles)
    sine_part = -window_taper[:, None] * jnp.sin(angles)
    return jnp.concatenate([cosine, sine_part], axis=1).astype(jnp.bfloat16)

def whiten(spectra, quality):
    nbins = spectra.shape[-1] // 2
    real_part = spectra[..., :nbins]
    imag_part = spectra[..., nbins:]
    band_rms = jnp.sqrt(lax.optimization_barrier(jnp.mean(spectra * spectra, axis=-1, keepdims=True)) + 1e-05)
    magnitude = jnp.sqrt(real_part * real_part + imag_part * imag_part)
    divisor = jnp.maximum(magnitude, 0.25 * band_rms)
    scaled = jnp.concatenate([real_part / divisor, imag_part / divisor], axis=-1)
    return (quality.astype(jnp.float32)[:, None] * scaled).astype(jnp.bfloat16)

def rotate(white, bin_ids, lag_shift, length):
    nbins = white.shape[-1] // 2
    phase_index = bin_ids * lag_shift % length
    angles = TWO_PI / length * phase_index.astype(jnp.float32)
    cosine = jnp.cos(angles)
    sine_part = jnp.sin(angles)
    real_part = white[..., :nbins].astype(jnp.float32)
    imag_part = white[..., nbins:].astype(jnp.float32)
    turned = jnp.concatenate([real_part * cosine + imag_part * sine_part, imag_part * cosine - real_part * sine_part], axis=-1)
    return turned.astype(jnp.bfloat16)

def reference(traces, quality_mask, band_bins):
    table = band_table(jnp.arange(W, dtype=jnp.int32), band_bins, W)
    spectra = jnp.stack([jnp.dot(traces[window], table, preferred_element_type=jnp.float32) for window in range(NWIN)])
    white = whiten(spectra, quality_mask)
    rows_dev = C // N_ROW
    per_dev = C // (N_ROW * N_COL)
    col_dev = C // N_COL
    places = jnp.arange(C, dtype=jnp.int32)
    perm = col_dev * (places % rows_dev // per_dev) + per_dev * (places // rows_dev) + places % per_dev
    row_spectra = white[:, perm, :]
    scale = 1.0 / math.sqrt(NWIN * K)
    results = []
    for lag_index in range(LAGS):
        lag_shift = (lag_index - LAGS // 2) * LAG_STEP
        rotated = rotate(row_spectra, band_bins, lag_shift, W)
        summed = jnp.zeros((C, C), jnp.float32)
        for window in range(NWIN):
            summed = summed + jnp.dot(rotated[window], white[window].T, preferred_element_type=jnp.float32)
        results.append(summed * scale)
    return jnp.stack(results)
```

```python
import functools
import math

import jax
import jax.numpy as jnp
from jax import lax
from jax.experimental import pallas as pl
from jax.experimental.pallas import tpu as pltpu
from jax.sharding import PartitionSpec as P

W = 16384
LAGS = 4
LAG_STEP = 50
TWO_PI = 2.0 * math.pi

F32 = jnp.float32
BF16 = jnp.bfloat16
VMEM_LIMIT = 56 * 1024 * 1024
FINE = 64


def band_table(sample_times, bin_ids, length):
    window_taper = 0.5 - 0.5 * jnp.cos(TWO_PI / length * sample_times.astype(F32))
    phase_index = sample_times[:, None] * bin_ids[None, :] % length
    angles = TWO_PI / length * phase_index.astype(F32)
    cosine = window_taper[:, None] * jnp.cos(angles)
    sine_part = -window_taper[:, None] * jnp.sin(angles)
    return jnp.concatenate([cosine, sine_part], axis=1).astype(BF16)


def whiten(spectra, quality):
    nbins = spectra.shape[-1] // 2
    real_part = spectra[..., :nbins]
    imag_part = spectra[..., nbins:]
    band_rms = jnp.sqrt(jnp.mean(spectra * spectra, axis=-1, keepdims=True) + 1e-05)
    magnitude = jnp.sqrt(real_part * real_part + imag_part * imag_part)
    divisor = jnp.maximum(magnitude, 0.25 * band_rms)
    scaled = jnp.concatenate([real_part / divisor, imag_part / divisor], axis=-1)
    return (quality.astype(F32)[:, None] * scaled).astype(BF16)


def rotate(white, bin_ids, lag_shift, length):
    nbins = white.shape[-1] // 2
    phase_index = bin_ids * lag_shift % length
    angles = TWO_PI / length * phase_index.astype(F32)
    cosine = jnp.cos(angles)
    sine_part = jnp.sin(angles)
    real_part = white[..., :nbins].astype(F32)
    imag_part = white[..., nbins:].astype(F32)
    turned = jnp.concatenate(
        [real_part * cosine + imag_part * sine_part, imag_part * cosine - real_part * sine_part],
        axis=-1,
    )
    return turned.astype(BF16)


def pair_products(row_spectra, column_spectra, bin_ids, length):
    results = []
    for lag_index in range(LAGS):
        lag_shift = (lag_index - LAGS // 2) * LAG_STEP
        rotated = rotate(row_spectra, bin_ids, lag_shift, length)
        results.append(
            jnp.einsum("wpk,wqk->pq", rotated, column_spectra, preferred_element_type=F32)
        )
    return jnp.stack(results)


def local_plain(traces, quality_mask, band_bins):
    nbins = band_bins.shape[0]
    windows_here = traces.shape[0]
    samples_here = traces.shape[2]
    sample_times = lax.axis_index("row") * samples_here + jnp.arange(samples_here, dtype=jnp.int32)
    table = band_table(sample_times, band_bins, W)
    partial_value = jnp.einsum("wct,tk->wck", traces, table, preferred_element_type=F32)
    spectra_all = lax.psum(partial_value, "row")
    column_spectra = whiten(spectra_all, quality_mask)
    local_channels = traces.shape[1] // lax.axis_size("row")
    white = lax.dynamic_slice_in_dim(
        column_spectra, lax.axis_index("row") * local_channels, local_channels, 1
    )
    row_spectra = lax.all_gather(white, "col", axis=1, tiled=True)
    scale = 1.0 / math.sqrt(lax.axis_size("sub") * windows_here * nbins)
    partial_products = pair_products(row_spectra, column_spectra, band_bins, W)
    summed = lax.psum_scatter(partial_products, "sub", scatter_dimension=2, tiled=True)
    return summed * scale


def fill_table(first_sample, bins_ref, table_ref, coarse_ref):
    nbins = bins_ref.shape[1]
    runs = table_ref.shape[0] // FINE
    bins = bins_ref[...]

    def turn(ids, times):
        angles = TWO_PI / W * ((ids * times) & (W - 1)).astype(F32)
        return jnp.cos(angles), jnp.sin(angles)

    fine_times = lax.broadcasted_iota(jnp.int32, (FINE, nbins), 0)
    coarse_times = first_sample + FINE * lax.broadcasted_iota(jnp.int32, (runs, nbins), 0)
    cos_f, sin_f = turn(bins, fine_times)
    cos_h, sin_h = turn(1, fine_times)
    for place, value in enumerate(turn(bins, coarse_times) + turn(1, coarse_times)):
        coarse_ref[place] = value

    @pl.loop(0, runs)
    def _(a):
        cos_c, sin_c, cos_g, sin_g = (coarse_ref[i, pl.ds(a, 1), :] for i in range(4))
        taper = 0.5 - 0.5 * (cos_g * cos_h - sin_g * sin_h)
        rows = pl.ds(pl.multiple_of(a * FINE, FINE), FINE)
        table_ref[rows, :nbins] = (taper * (cos_c * cos_f - sin_c * sin_f)).astype(BF16)
        table_ref[rows, nbins:] = (-taper * (sin_c * cos_f + cos_c * sin_f)).astype(BF16)


def spectra_kernel(with_table, split, block, where_ref, bins_or_table, traces_ref, *rest):
    if with_table:
        right_ref, left_ref, table_ref, right_buf, left_buf, sems, coarse_ref = rest
    else:
        right_ref, left_ref, right_buf, left_buf, sems = rest
        table_ref = bins_or_table
    windows = traces_ref.shape[0]
    right_start = pl.multiple_of(where_ref[1] * block, 128)
    left_start = pl.multiple_of(where_ref[2] * block + split, 128)
    copies = []
    for w in range(windows):
        copies.append(
            pltpu.make_async_copy(
                traces_ref.at[w, pl.ds(right_start, split), :], right_buf.at[w], sems.at[0, w]
            )
        )
        copies.append(
            pltpu.make_async_copy(
                traces_ref.at[w, pl.ds(left_start, block - split), :], left_buf.at[w], sems.at[1, w]
            )
        )
    for copy in copies:
        copy.start()
    if with_table:
        fill_table(where_ref[0], bins_or_table, table_ref, coarse_ref)
    width = table_ref.shape[1]
    for w in range(windows):
        for side, (buf, out) in enumerate(((right_buf, right_ref), (left_buf, left_ref))):
            copies[2 * w + side].wait()
            out[:, w * width : (w + 1) * width] = jnp.dot(
                buf[w], table_ref[...], preferred_element_type=F32
            ).astype(out.dtype)


def spectra_call(where, bins_or_table, traces, split, block, with_table, dtype):
    windows, _, samples = traces.shape
    nbins = bins_or_table.shape[1] if with_table else bins_or_table.shape[1] // 2
    lanes = windows * 2 * nbins
    vmem = pl.BlockSpec(memory_space=pltpu.VMEM)
    out_shape = [
        jax.ShapeDtypeStruct((split, lanes), dtype),
        jax.ShapeDtypeStruct((block - split, lanes), dtype),
    ]
    scratch = [
        pltpu.VMEM((windows, split, samples), BF16),
        pltpu.VMEM((windows, block - split, samples), BF16),
        pltpu.SemaphoreType.DMA((2, windows)),
    ]
    if with_table:
        out_shape.append(jax.ShapeDtypeStruct((samples, 2 * nbins), BF16))
        scratch.append(pltpu.VMEM((4, samples // FINE, nbins), F32))
    return pl.pallas_call(
        functools.partial(spectra_kernel, with_table, split, block),
        out_shape=out_shape,
        in_specs=[
            pl.BlockSpec(memory_space=pltpu.SMEM),
            vmem,
            pl.BlockSpec(memory_space=pl.ANY),
        ],
        out_specs=[vmem] * len(out_shape),
        scratch_shapes=scratch,
        compiler_params=pltpu.CompilerParams(vmem_limit_bytes=VMEM_LIMIT),
        cost_estimate=pl.CostEstimate(
            flops=2 * block * lanes * samples,
            bytes_accessed=2 * windows * block * samples + 4 * block * lanes,
            transcendentals=0,
        ),
        name="spectra",
    )(where, bins_or_table, traces)


def whiten_kernel(got_r, got_l, own_r, own_l, quality, white, white_r, white_l):
    split = got_r.shape[0]
    lanes = got_r.shape[1]
    nbins = lanes // 4
    for got, own, out, first in ((got_r, own_r, white_r, 0), (got_l, own_l, white_l, split)):
        rows = got.shape[0]
        mask = quality[first : first + rows, :]
        for w in range(2):
            low = w * 2 * nbins
            real = got[:, low : low + nbins].astype(F32) + own[:, low : low + nbins]
            high = low + nbins
            imag = got[:, high : high + nbins].astype(F32) + own[:, high : high + nbins]
            power = real * real + imag * imag
            mean = jnp.sum(power, axis=1, keepdims=True) * (0.5 / nbins)
            factor = mask * jnp.minimum(lax.rsqrt(power), 4.0 * lax.rsqrt(mean + 1e-05))
            real = (real * factor).astype(BF16)
            imag = (imag * factor).astype(BF16)
            out[:, low : low + nbins] = real
            out[:, high : high + nbins] = imag
            white[first : first + rows, low : low + nbins] = real
            white[first : first + rows, high : high + nbins] = imag


def whiten_call(got_r, got_l, own_r, own_l, quality):
    vmem = pl.BlockSpec(memory_space=pltpu.VMEM)
    split, lanes = got_r.shape
    rest = got_l.shape[0]
    return pl.pallas_call(
        whiten_kernel,
        out_shape=[
            jax.ShapeDtypeStruct((split + rest, lanes), BF16),
            jax.ShapeDtypeStruct((split, lanes), BF16),
            jax.ShapeDtypeStruct((rest, lanes), BF16),
        ],
        in_specs=[vmem] * 5,
        out_specs=[vmem] * 3,
        compiler_params=pltpu.CompilerParams(vmem_limit_bytes=VMEM_LIMIT),
        cost_estimate=pl.CostEstimate(
            flops=12 * (split + rest) * lanes,
            bytes_accessed=12 * (split + rest) * lanes,
            transcendentals=(split + rest) * lanes // 2,
        ),
        name="whiten",
    )(got_r, got_l, own_r, own_l, quality)


def rotate_kernel(cos_ref, sin_ref, near_o, near_t, far_o, far_t, out):
    nbins = cos_ref.shape[2]
    cosine = cos_ref[0]
    sine = sin_ref[0]
    half = near_o.shape[1]
    for side, (o_ref, t_ref) in enumerate(((near_o, near_t), (far_o, far_t))):

        @pl.when(pl.program_id(0) == side)
        def _():
            for ref, base in ((o_ref, 0), (t_ref, half)):
                for w in range(2):
                    low = w * 2 * nbins
                    high = low + nbins
                    real = ref[:, low : low + nbins].astype(F32)
                    imag = ref[:, high : high + nbins].astype(F32)
                    out[0, :, base + low : base + low + nbins] = (
                        real * cosine + imag * sine
                    ).astype(BF16)
                    out[0, :, base + high : base + high + nbins] = (
                        imag * cosine - real * sine
                    ).astype(BF16)


def rotate_call(cosine, sine, near_o, near_t, far_o, far_t):
    block, half = near_o.shape
    nbins = cosine.shape[2]
    whole = pl.BlockSpec((block, half), lambda x, l: (0, 0))
    lag = pl.BlockSpec((1, 1, nbins), lambda x, l: (l, 0, 0))
    return pl.pallas_call(
        rotate_kernel,
        grid=(2, LAGS),
        out_shape=jax.ShapeDtypeStruct((2 * LAGS, block, 2 * half), BF16),
        in_specs=[lag, lag] + [whole] * 4,
        out_specs=pl.BlockSpec((1, block, 2 * half), lambda x, l: (x * LAGS + l, 0, 0)),
        compiler_params=pltpu.CompilerParams(vmem_limit_bytes=VMEM_LIMIT),
        cost_estimate=pl.CostEstimate(
            flops=6 * 2 * LAGS * block * 2 * half,
            bytes_accessed=2 * 2 * LAGS * block * 2 * half,
            transcendentals=0,
        ),
        name="rotate",
    )(cosine, sine, near_o, near_t, far_o, far_t)


def product_kernel(gather, scale, has_base, *refs):
    info, rows = refs[:2]
    out = refs[-4]
    columns, tiles, sems = refs[-3:]
    parts = refs[2 : -5 if has_base else -4]
    step = pl.program_id(0)
    steps = pl.num_programs(0)
    block = rows.shape[1]
    width = columns.shape[0]
    start = pl.multiple_of(info[0], 128)

    def place(index):
        side = lax.div(index, LAGS)
        first = pl.multiple_of(info[1 + side] * block, 128)
        return pltpu.make_async_copy(
            tiles.at[lax.rem(index, 2)],
            out.at[lax.rem(index, LAGS), pl.ds(first, block), pl.ds(start, width)],
            sems.at[lax.rem(index, 2)],
        )

    @pl.when(step == 0)
    def _():
        gather(info, parts, columns)

    @pl.when(step >= 2)
    def _():
        place(step - 2).wait()

    tiles[lax.rem(step, 2)] = scale * lax.dot_general(
        rows[0], columns[...], (((1,), (1,)), ((), ())), preferred_element_type=F32
    )
    place(step).start()

    @pl.when(step == steps - 1)
    def _():
        place(step - 1).wait()
        place(step).wait()


def product_call(info, rows, parts, gather, width, scale, base, out_shape):
    steps, block, depth = rows.shape
    vmem = pl.BlockSpec(memory_space=pltpu.VMEM)
    anywhere = pl.BlockSpec(memory_space=pl.ANY)
    operands = [info, rows] + list(parts)
    in_specs = [
        pl.BlockSpec(memory_space=pltpu.SMEM),
        pl.BlockSpec((1, block, depth), lambda s: (s, 0, 0)),
    ] + [vmem] * len(parts)
    aliases = {}
    if base is not None:
        aliases = {len(operands): 0}
        operands.append(base)
        in_specs.append(anywhere)
    return pl.pallas_call(
        functools.partial(product_kernel, gather, scale, base is not None),
        grid=(steps,),
        out_shape=out_shape,
        in_specs=in_specs,
        out_specs=anywhere,
        scratch_shapes=[
            pltpu.VMEM((width, depth), BF16),
            pltpu.VMEM((2, block, width), F32),
            pltpu.SemaphoreType.DMA((2,)),
        ],
        input_output_aliases=aliases,
        compiler_params=pltpu.CompilerParams(vmem_limit_bytes=VMEM_LIMIT),
        cost_estimate=pl.CostEstimate(
            flops=2 * steps * block * depth * width,
            bytes_accessed=steps * block * (2 * depth + 4 * width),
            transcendentals=0,
        ),
        name="products",
    )(*operands)


def gather_full(split, info, parts, columns):
    own_o, own_t, right_o, right_t, left_o, left_t = parts
    half = own_o.shape[1]

    @pl.when(info[3] == 1)
    def _():
        columns[:, :half] = own_o[...]
        columns[:, half:] = own_t[...]

    @pl.when(info[3] == 0)
    def _():
        columns[:split, :half] = right_o[...]
        columns[:split, half:] = right_t[...]
        columns[split:, :half] = left_o[...]
        columns[split:, half:] = left_t[...]


def gather_first(info, parts, columns):
    right_o, right_t, left_o, left_t = parts
    half = right_o.shape[1]
    width = columns.shape[0]

    @pl.when(info[3] == 1)
    def _():
        columns[:, :half] = right_o[:width, :]
        columns[:, half:] = right_t[:width, :]

    @pl.when(info[3] == 0)
    def _():
        columns[:, :half] = left_o[...]
        columns[:, half:] = left_t[...]


def gather_last(overlap, info, parts, columns):
    early_o, early_t, right_o, right_t, left_o, left_t = parts
    half = right_o.shape[1]
    split = right_o.shape[0]

    @pl.when(info[3] == 1)
    def _():
        columns[:overlap, :half] = early_o[split - overlap :, :]
        columns[:overlap, half:] = early_t[split - overlap :, :]
        columns[overlap:, :half] = left_o[...]
        columns[overlap:, half:] = left_t[...]

    @pl.when(info[3] == 0)
    def _():
        columns[:, :half] = right_o[...]
        columns[:, half:] = right_t[...]


def local_rings(traces, quality_mask, band_bins):
    n = lax.axis_size("row")
    windows, channels, samples = traces.shape
    nbins = band_bins.shape[0]
    block = channels // n
    split = (block // 128 + 1) // 2 * 128
    rest = block - split
    z = lax.axis_index("row")
    x = lax.axis_index("col")
    c = lax.axis_index("sub")
    to_right = [(i, (i + 1) % n) for i in range(n)]
    to_left = [(i, (i - 1) % n) for i in range(n)]
    i32 = jnp.int32

    def where(k):
        return jnp.stack([z * samples, (z - 1 - k) % n, (z + 1 + k) % n]).astype(i32)

    own = []
    right, left, table = spectra_call(
        where(0), band_bins[None, :], traces, split, block, True, BF16
    )
    for k in range(1, n):
        own.append(spectra_call(where(k), table, traces, split, block, False, F32))
    for k in range(n - 1):
        right = lax.ppermute(right, "row", to_right)
        left = lax.ppermute(left, "row", to_left)
        if k < n - 2:
            right = (right.astype(F32) + own[k][0]).astype(BF16)
            left = (left.astype(F32) + own[k][1]).astype(BF16)
    quality = lax.dynamic_slice_in_dim(quality_mask, z * block, block).astype(F32)[:, None]
    white, white_r, white_l = whiten_call(right, left, *own[-1], quality)

    def core_of(b):
        return (b % n) * 2 // n

    def pairs(step, move, cross):
        found = []
        for i in range(n):
            core = core_of(i - step * move)
            source = 1 - core if cross else core
            found.append((i * 2 + source, (i + move) % n * 2 + core))
        return found

    axes = ("row", "sub")
    r0 = [lax.ppermute(white_r, axes, pairs(0, 1, cross)) for cross in (False, True)]
    l0 = [lax.ppermute(white_l, axes, pairs(0, -1, cross)) for cross in (False, True)]
    r1 = [lax.ppermute(part, axes, pairs(1, 1, False)) for part in r0]
    l1 = [lax.ppermute(part, axes, pairs(1, -1, False)) for part in l0]
    r2 = [lax.ppermute(part, axes, pairs(2, 1, False)) for part in r1]
    l2 = [lax.ppermute(part, axes, pairs(2, -1, False)) for part in l1]

    swap = [(0, 1), (1, 0)]
    white_t = lax.ppermute(white, "sub", swap)
    far = lax.ppermute(white, "col", swap)
    far_t = lax.ppermute(far, "sub", swap)
    shifts = jnp.array([(lag - LAGS // 2) * LAG_STEP for lag in range(LAGS)], i32)
    angles = TWO_PI / W * (band_bins[None, :] * shifts[:, None] % W).astype(F32)
    rows = rotate_call(
        jnp.cos(angles)[:, None, :], jnp.sin(angles)[:, None, :], white, white_t, far, far_t
    )

    per_core = n // 2
    owner = z // per_core == c
    from_right = (z - 1) % n // per_core == c
    full = jnp.where(owner, z, (z + 2) % n) - per_core * c
    other = 1 - full
    scale = 1.0 / math.sqrt(2 * windows * nbins)
    out_shape = jax.ShapeDtypeStruct((LAGS, 2 * block, per_core * block), F32)

    def info(start, flag):
        return jnp.stack([start, x, 1 - x, flag]).astype(i32)

    overlap = split - rest
    result = product_call(
        info(full * block, owner), rows, [white, white_t] + r1 + l1,
        functools.partial(gather_full, split), block, scale, None, out_shape,
    )
    result = product_call(
        info(other * block + jnp.where(from_right, 0, split), from_right), rows, r0 + l0,
        gather_first, rest, scale, result, out_shape,
    )
    return product_call(
        info(other * block + jnp.where(from_right, rest, 0), from_right), rows, r0 + r2 + l2,
        functools.partial(gather_last, overlap), split, scale, result, out_shape,
    )


def solution(mesh):
    in_specs = (P(("group", "sub"), "col", "row"), P("col"), P())
    out_specs = P("group", "row", ("col", "sub"))
    rings = (mesh.shape["row"], mesh.shape["col"], mesh.shape["sub"]) == (4, 2, 2)
    return jax.shard_map(
        local_rings if rings else local_plain,
        mesh=mesh, in_specs=in_specs, out_specs=out_specs, check_vma=False,
    )
```

```python
import functools
import math

import jax
import jax.numpy as jnp
from jax import lax
from jax.experimental import pallas as pl
from jax.experimental.pallas import tpu as pltpu
from jax.sharding import PartitionSpec as P

W = 16384
LAGS = 4
LAG_STEP = 50
TWO_PI = 2.0 * math.pi

F32 = jnp.float32
BF16 = jnp.bfloat16
MIB = 1024 * 1024
SPECTRA_VMEM = 18 * MIB
SMALL_VMEM = 8 * MIB
PRODUCT_VMEM = 12 * MIB
SMALL = pl.CostEstimate(flops=1000, bytes_accessed=1000, transcendentals=0)
FINE = 64


def band_table(sample_times, bin_ids, length):
    window_taper = 0.5 - 0.5 * jnp.cos(TWO_PI / length * sample_times.astype(F32))
    phase_index = sample_times[:, None] * bin_ids[None, :] % length
    angles = TWO_PI / length * phase_index.astype(F32)
    cosine = window_taper[:, None] * jnp.cos(angles)
    sine_part = -window_taper[:, None] * jnp.sin(angles)
    return jnp.concatenate([cosine, sine_part], axis=1).astype(BF16)


def whiten(spectra, quality):
    nbins = spectra.shape[-1] // 2
    real_part = spectra[..., :nbins]
    imag_part = spectra[..., nbins:]
    band_rms = jnp.sqrt(jnp.mean(spectra * spectra, axis=-1, keepdims=True) + 1e-05)
    magnitude = jnp.sqrt(real_part * real_part + imag_part * imag_part)
    divisor = jnp.maximum(magnitude, 0.25 * band_rms)
    scaled = jnp.concatenate([real_part / divisor, imag_part / divisor], axis=-1)
    return (quality.astype(F32)[:, None] * scaled).astype(BF16)


def rotate(white, bin_ids, lag_shift, length):
    nbins = white.shape[-1] // 2
    phase_index = bin_ids * lag_shift % length
    angles = TWO_PI / length * phase_index.astype(F32)
    cosine = jnp.cos(angles)
    sine_part = jnp.sin(angles)
    real_part = white[..., :nbins].astype(F32)
    imag_part = white[..., nbins:].astype(F32)
    turned = jnp.concatenate(
        [real_part * cosine + imag_part * sine_part, imag_part * cosine - real_part * sine_part],
        axis=-1,
    )
    return turned.astype(BF16)


def pair_products(row_spectra, column_spectra, bin_ids, length):
    results = []
    for lag_index in range(LAGS):
        lag_shift = (lag_index - LAGS // 2) * LAG_STEP
        rotated = rotate(row_spectra, bin_ids, lag_shift, length)
        results.append(
            jnp.einsum("wpk,wqk->pq", rotated, column_spectra, preferred_element_type=F32)
        )
    return jnp.stack(results)


def local_plain(traces, quality_mask, band_bins):
    nbins = band_bins.shape[0]
    windows_here = traces.shape[0]
    samples_here = traces.shape[2]
    sample_times = lax.axis_index("row") * samples_here + jnp.arange(samples_here, dtype=jnp.int32)
    table = band_table(sample_times, band_bins, W)
    partial_value = jnp.einsum("wct,tk->wck", traces, table, preferred_element_type=F32)
    spectra_all = lax.psum(partial_value, "row")
    column_spectra = whiten(spectra_all, quality_mask)
    local_channels = traces.shape[1] // lax.axis_size("row")
    white = lax.dynamic_slice_in_dim(
        column_spectra, lax.axis_index("row") * local_channels, local_channels, 1
    )
    row_spectra = lax.all_gather(white, "col", axis=1, tiled=True)
    scale = 1.0 / math.sqrt(lax.axis_size("sub") * windows_here * nbins)
    partial_products = pair_products(row_spectra, column_spectra, band_bins, W)
    summed = lax.psum_scatter(partial_products, "sub", scatter_dimension=2, tiled=True)
    return summed * scale


def fill_table(first_sample, bins_ref, table_ref, coarse_ref, halfway):
    nbins = bins_ref.shape[1]
    runs = table_ref.shape[0] // FINE
    bins = bins_ref[...]

    def turn(ids, times):
        phase = (ids * times) & (W - 1)
        quarter = (phase + W // 8) // (W // 4)
        angle = (TWO_PI / W) * (phase - quarter * (W // 4)).astype(F32)
        square = angle * angle
        sine = jnp.full_like(square, 1.0 / 362880)
        for term in (-1.0 / 5040, 1.0 / 120, -1.0 / 6, 1.0):
            sine = sine * square + term
        sine = sine * angle
        cosine = jnp.full_like(square, -1.0 / 3628800)
        for term in (1.0 / 40320, -1.0 / 720, 1.0 / 24, -0.5, 1.0):
            cosine = cosine * square + term
        odd = (quarter & 1) == 1
        cosine, sine = jnp.where(odd, sine, cosine), jnp.where(odd, cosine, sine)
        cosine = jnp.where(((quarter + 1) & 2) == 2, -cosine, cosine)
        sine = jnp.where((quarter & 2) == 2, -sine, sine)
        return cosine, sine

    fine_times = lax.broadcasted_iota(jnp.int32, (FINE, nbins), 0)
    coarse_times = first_sample + FINE * lax.broadcasted_iota(jnp.int32, (runs, nbins), 0)
    cos_f, sin_f = turn(bins, fine_times)
    cos_h, sin_h = turn(1, fine_times)
    for place, value in enumerate(turn(bins, coarse_times) + turn(1, coarse_times)):
        coarse_ref[place] = value

    def fill(a):
        cos_c, sin_c, cos_g, sin_g = (coarse_ref[i, pl.ds(a, 1), :] for i in range(4))
        taper = 0.5 - 0.5 * (cos_g * cos_h - sin_g * sin_h)
        rows = pl.ds(pl.multiple_of(a * FINE, FINE), FINE)
        table_ref[rows, :nbins] = (taper * (cos_c * cos_f - sin_c * sin_f)).astype(BF16)
        table_ref[rows, nbins:] = (-taper * (sin_c * cos_f + cos_c * sin_f)).astype(BF16)

    pl.loop(0, runs // 2)(fill)
    halfway()
    pl.loop(runs // 2, runs)(fill)


def spectra_kernel(with_table, firsts, sizes, block, where_ref, bins_or_table, traces_ref, *rest):
    sides = len(sizes)
    outs, bufs, sems = rest[:sides], rest[-sides - 1 : -1], rest[-1]
    windows = traces_ref.shape[0]
    copies = []
    for w in range(windows):
        for i, size in enumerate(sizes):
            start = pl.multiple_of(where_ref[1 + i] * block + firsts[i], 128)
            copies.append(
                pltpu.make_async_copy(
                    traces_ref.at[w, pl.ds(start, size), :], bufs[i].at[w], sems.at[i, w]
                )
            )
    copies[0].start()
    if with_table:
        table_ref, coarse_ref = rest[sides : sides + 2]
        fill_table(where_ref[0], bins_or_table, table_ref, coarse_ref, copies[1].start)
    else:
        table_ref = bins_or_table
        copies[1].start()
    width = table_ref.shape[1]
    for index, copy in enumerate(copies):
        w, i = divmod(index, sides)
        copy.wait()
        if index + 2 < len(copies):
            copies[index + 2].start()
        outs[i][:, w * width : (w + 1) * width] = jnp.dot(
            bufs[i][w], table_ref[...], preferred_element_type=F32
        ).astype(outs[i].dtype)


def spectra_call(where, bins_or_table, traces, firsts, sizes, block, with_table, dtype):
    windows, _, samples = traces.shape
    nbins = bins_or_table.shape[1] if with_table else bins_or_table.shape[1] // 2
    lanes = windows * 2 * nbins
    vmem = pl.BlockSpec(memory_space=pltpu.VMEM)
    out_shape = [jax.ShapeDtypeStruct((size, lanes), dtype) for size in sizes]
    scratch = []
    if with_table:
        out_shape.append(jax.ShapeDtypeStruct((samples, 2 * nbins), BF16))
        scratch.append(pltpu.VMEM((4, samples // FINE, nbins), F32))
    scratch += [pltpu.VMEM((windows, size, samples), BF16) for size in sizes]
    scratch.append(pltpu.SemaphoreType.DMA((len(sizes), windows)))
    return pl.pallas_call(
        functools.partial(spectra_kernel, with_table, firsts, sizes, block),
        out_shape=out_shape,
        in_specs=[
            pl.BlockSpec(memory_space=pltpu.SMEM),
            vmem,
            pl.BlockSpec(memory_space=pl.ANY),
        ],
        out_specs=[vmem] * len(out_shape),
        scratch_shapes=scratch,
        compiler_params=pltpu.CompilerParams(vmem_limit_bytes=SPECTRA_VMEM),
        cost_estimate=SMALL,
        name="spectra",
    )(where, bins_or_table, traces)


def whiten_kernel(got_r, got_l, own_r, own_l, quality, white, white_r, white_l):
    split = got_r.shape[0]
    lanes = got_r.shape[1]
    nbins = lanes // 4
    for got, own, out, first in ((got_r, own_r, white_r, 0), (got_l, own_l, white_l, split)):
        rows = got.shape[0]
        mask = quality[first : first + rows, :]
        for w in range(2):
            low = w * 2 * nbins
            real = got[:, low : low + nbins].astype(F32) + own[:, low : low + nbins]
            high = low + nbins
            imag = got[:, high : high + nbins].astype(F32) + own[:, high : high + nbins]
            power = real * real + imag * imag
            mean = jnp.sum(power, axis=1, keepdims=True) * (0.5 / nbins)
            factor = mask * jnp.minimum(lax.rsqrt(power), 4.0 * lax.rsqrt(mean + 1e-05))
            real = (real * factor).astype(BF16)
            imag = (imag * factor).astype(BF16)
            out[:, low : low + nbins] = real
            out[:, high : high + nbins] = imag
            white[first : first + rows, low : low + nbins] = real
            white[first : first + rows, high : high + nbins] = imag


def whiten_call(got_r, got_l, own_r, own_l, quality):
    vmem = pl.BlockSpec(memory_space=pltpu.VMEM)
    split, lanes = got_r.shape
    rest = got_l.shape[0]
    return pl.pallas_call(
        whiten_kernel,
        out_shape=[
            jax.ShapeDtypeStruct((split + rest, lanes), BF16),
            jax.ShapeDtypeStruct((split, lanes), BF16),
            jax.ShapeDtypeStruct((rest, lanes), BF16),
        ],
        in_specs=[vmem] * 5,
        out_specs=[vmem] * 3,
        compiler_params=pltpu.CompilerParams(vmem_limit_bytes=SMALL_VMEM),
        cost_estimate=SMALL,
        name="whiten",
    )(got_r, got_l, own_r, own_l, quality)


def rotate_kernel(cos_ref, sin_ref, near_o, near_t, far_o, far_t, out):
    nbins = cos_ref.shape[2]
    cosine = cos_ref[0]
    sine = sin_ref[0]
    half = near_o.shape[1]
    for side, (o_ref, t_ref) in enumerate(((near_o, near_t), (far_o, far_t))):

        @pl.when(pl.program_id(0) == side)
        def _():
            for ref, base in ((o_ref, 0), (t_ref, half)):
                for w in range(2):
                    low = w * 2 * nbins
                    high = low + nbins
                    real = ref[:, low : low + nbins].astype(F32)
                    imag = ref[:, high : high + nbins].astype(F32)
                    out[0, :, base + low : base + low + nbins] = (
                        real * cosine + imag * sine
                    ).astype(BF16)
                    out[0, :, base + high : base + high + nbins] = (
                        imag * cosine - real * sine
                    ).astype(BF16)


def rotate_call(cosine, sine, near_o, near_t, far_o, far_t):
    block, half = near_o.shape
    nbins = cosine.shape[2]
    whole = pl.BlockSpec((block, half), lambda x, l: (0, 0))
    lag = pl.BlockSpec((1, 1, nbins), lambda x, l: (l, 0, 0))
    return pl.pallas_call(
        rotate_kernel,
        grid=(2, LAGS),
        out_shape=jax.ShapeDtypeStruct((2 * LAGS, block, 2 * half), BF16),
        in_specs=[lag, lag] + [whole] * 4,
        out_specs=pl.BlockSpec((1, block, 2 * half), lambda x, l: (x * LAGS + l, 0, 0)),
        compiler_params=pltpu.CompilerParams(vmem_limit_bytes=SMALL_VMEM),
        cost_estimate=SMALL,
        name="rotate",
    )(cosine, sine, near_o, near_t, far_o, far_t)


def product_kernel(gather, scale, has_base, *refs):
    info, rows = refs[:2]
    out, columns, tiles, sems = refs[-4:]
    parts = refs[2 : -5 if has_base else -4]
    steps, block, _ = rows.shape
    width = columns.shape[0]
    start = pl.multiple_of(info[2], 128)
    gather(info, parts, columns)

    def place(index):
        side = lax.div(index, LAGS)
        slot = lax.rem(index, 2)
        first = pl.multiple_of(info[side] * block, 128)
        return pltpu.make_async_copy(
            tiles.at[slot],
            out.at[lax.rem(index, LAGS), pl.ds(first, block), pl.ds(start, width)],
            sems.at[slot],
        )

    @pl.loop(0, steps)
    def _(step):
        @pl.when(step >= 2)
        def _():
            place(step - 2).wait()

        tiles[lax.rem(step, 2)] = scale * lax.dot_general(
            rows[step], columns[...], (((1,), (1,)), ((), ())), preferred_element_type=F32
        )
        place(step).start()

    place(steps - 2).wait()
    place(steps - 1).wait()


def product_call(info, rows, parts, gather, width, scale, base, out_shape):
    steps, block, depth = rows.shape
    vmem = pl.BlockSpec(memory_space=pltpu.VMEM)
    anywhere = pl.BlockSpec(memory_space=pl.ANY)
    operands = [info, rows] + list(parts)
    in_specs = [pl.BlockSpec(memory_space=pltpu.SMEM)] + [vmem] * (1 + len(parts))
    aliases = {}
    if base is not None:
        aliases = {len(operands): 0}
        operands.append(base)
        in_specs.append(anywhere)
    return pl.pallas_call(
        functools.partial(product_kernel, gather, scale, base is not None),
        out_shape=out_shape,
        in_specs=in_specs,
        out_specs=anywhere,
        scratch_shapes=[
            pltpu.VMEM((width, depth), BF16),
            pltpu.VMEM((2, block, width), F32),
            pltpu.SemaphoreType.DMA((2,)),
        ],
        input_output_aliases=aliases,
        compiler_params=pltpu.CompilerParams(vmem_limit_bytes=PRODUCT_VMEM),
        cost_estimate=SMALL,
        name="products",
    )(*operands)


def gather_full(split, info, parts, columns):
    own_o, own_t, right, left = parts
    half = own_o.shape[1]

    @pl.when(info[3] == 1)
    def _():
        columns[:, :half] = own_o[...]
        columns[:, half:] = own_t[...]

    @pl.when(info[3] == 0)
    def _():
        columns[:split, :] = right[...]
        columns[split:, :] = left[...]


def gather_first(info, parts, columns):
    right, left = parts

    @pl.when(info[3] == 1)
    def _():
        columns[...] = right[: columns.shape[0], :]

    @pl.when(info[3] == 0)
    def _():
        columns[...] = left[...]


def gather_last(overlap, info, parts, columns):
    early, right, left = parts

    @pl.when(info[3] == 1)
    def _():
        columns[:overlap, :] = early[early.shape[0] - overlap :, :]
        columns[overlap:, :] = left[...]

    @pl.when(info[3] == 0)
    def _():
        columns[...] = right[...]


def local_rings(traces, quality_mask, band_bins):
    n = lax.axis_size("row")
    windows, channels, samples = traces.shape
    nbins = band_bins.shape[0]
    block = channels // n
    split = (block // 128 + 1) // 2 * 128
    rest = block - split
    z = lax.axis_index("row")
    x = lax.axis_index("col")
    c = lax.axis_index("sub")
    to_right = [(i, (i + 1) % n) for i in range(n)]
    to_left = [(i, (i - 1) % n) for i in range(n)]
    i32 = jnp.int32

    def where(*blocks):
        return jnp.stack([z * samples, *(b % n for b in blocks)]).astype(i32)

    right, left, table = spectra_call(
        where(z - 1, z + 1), band_bins[None, :], traces, (0, split), (split, rest), block, True, BF16
    )
    for k in range(1, n):
        places = where(z - 1 - k, z + 1 + k)
        if k > 1:
            places, right, left = lax.optimization_barrier((places, right, left))
        own_r, own_l = spectra_call(
            places, table, traces, (0, split), (split, rest), block, False, F32
        )
        right = lax.ppermute(right, "row", to_right)
        left = lax.ppermute(left, "row", to_left)
        if k < n - 1:
            right = (right.astype(F32) + own_r).astype(BF16)
            left = (left.astype(F32) + own_l).astype(BF16)
    quality = lax.dynamic_slice_in_dim(quality_mask, z * block, block).astype(F32)[:, None]
    white, white_r, white_l = whiten_call(right, left, own_r, own_l, quality)

    def core_of(b):
        return (b % n) * 2 // n

    def pairs(step, move, cross):
        found = []
        for i in range(n):
            core = core_of(i - step * move)
            source = 1 - core if cross else core
            found.append((i * 2 + source, (i + move) % n * 2 + core))
        return found

    axes = ("row", "sub")
    swap = [(0, 1), (1, 0)]
    white_t = lax.ppermute(white, "sub", swap)
    r0 = [lax.ppermute(white_r, axes, pairs(0, 1, cross)) for cross in (False, True)]
    l0 = [lax.ppermute(white_l, axes, pairs(0, -1, cross)) for cross in (False, True)]
    r0, l0 = jnp.concatenate(r0, axis=1), jnp.concatenate(l0, axis=1)
    r1 = lax.ppermute(r0, axes, pairs(1, 1, False))
    l1 = lax.ppermute(l0, axes, pairs(1, -1, False))

    near, white_t = lax.optimization_barrier((white, white_t))
    far = lax.ppermute(near, "col", swap)
    far_t = lax.ppermute(far, "sub", swap)
    shifts = jnp.array([(lag - LAGS // 2) * LAG_STEP for lag in range(LAGS)], i32)
    angles = TWO_PI / W * (band_bins[None, :] * shifts[:, None] % W).astype(F32)
    rows = rotate_call(
        jnp.cos(angles)[:, None, :], jnp.sin(angles)[:, None, :], white, white_t, far, far_t
    )

    per_core = n // 2
    owner = z // per_core == c
    from_right = (z - 1) % n // per_core == c
    full = jnp.where(owner, z, (z + 2) % n) - per_core * c
    other = 1 - full
    scale = 1.0 / math.sqrt(2 * windows * nbins)
    out_shape = jax.ShapeDtypeStruct((LAGS, 2 * block, per_core * block), F32)

    first_start = other * block + jnp.where(from_right, 0, split)
    last_start = other * block + jnp.where(from_right, rest, 0)

    def info(start, flag):
        return jnp.stack([x, 1 - x, start, flag]).astype(i32)

    result = product_call(
        info(first_start, from_right), rows, [r0, l0], gather_first, rest, scale, None, out_shape
    )
    r1, l1, result = lax.optimization_barrier((r1, l1, result))
    r2 = lax.ppermute(r1, axes, pairs(2, 1, False))
    l2 = lax.ppermute(l1, axes, pairs(2, -1, False))
    result = product_call(
        info(full * block, owner), rows, [white, white_t, r1, l1],
        functools.partial(gather_full, split), block, scale, result, out_shape,
    )
    return product_call(
        info(last_start, from_right), rows, [r0, r2, l2],
        functools.partial(gather_last, split - rest), split, scale, result, out_shape,
    )


def solution(mesh):
    in_specs = (P(("group", "sub"), "col", "row"), P("col"), P())
    out_specs = P("group", "row", ("col", "sub"))
    rings = (mesh.shape["row"], mesh.shape["col"], mesh.shape["sub"]) == (4, 2, 2)
    return jax.shard_map(
        local_rings if rings else local_plain,
        mesh=mesh, in_specs=in_specs, out_specs=out_specs, check_vma=False,
    )
```

```python
import functools
import math

import jax
import jax.numpy as jnp
from jax import lax
from jax.experimental import pallas as pl
from jax.experimental.pallas import tpu as pltpu
from jax.sharding import PartitionSpec as P

W = 16384
LAGS = 4
LAG_STEP = 50
TWO_PI = 2.0 * math.pi

F32 = jnp.float32
BF16 = jnp.bfloat16
MIB = 1024 * 1024
SPECTRA_VMEM = 18 * MIB
SMALL_VMEM = 8 * MIB
PRODUCT_VMEM = 16 * MIB
SMALL = pl.CostEstimate(flops=1000, bytes_accessed=1000, transcendentals=0)
AHEAD = 3
ROWS_KEPT = 48
FINE = 64


def band_table(sample_times, bin_ids, length):
    window_taper = 0.5 - 0.5 * jnp.cos(TWO_PI / length * sample_times.astype(F32))
    phase_index = sample_times[:, None] * bin_ids[None, :] % length
    angles = TWO_PI / length * phase_index.astype(F32)
    cosine = window_taper[:, None] * jnp.cos(angles)
    sine_part = -window_taper[:, None] * jnp.sin(angles)
    return jnp.concatenate([cosine, sine_part], axis=1).astype(BF16)


def whiten(spectra, quality):
    nbins = spectra.shape[-1] // 2
    real_part = spectra[..., :nbins]
    imag_part = spectra[..., nbins:]
    band_rms = jnp.sqrt(jnp.mean(spectra * spectra, axis=-1, keepdims=True) + 1e-05)
    magnitude = jnp.sqrt(real_part * real_part + imag_part * imag_part)
    divisor = jnp.maximum(magnitude, 0.25 * band_rms)
    scaled = jnp.concatenate([real_part / divisor, imag_part / divisor], axis=-1)
    return (quality.astype(F32)[:, None] * scaled).astype(BF16)


def rotate(white, bin_ids, lag_shift, length):
    nbins = white.shape[-1] // 2
    phase_index = bin_ids * lag_shift % length
    angles = TWO_PI / length * phase_index.astype(F32)
    cosine = jnp.cos(angles)
    sine_part = jnp.sin(angles)
    real_part = white[..., :nbins].astype(F32)
    imag_part = white[..., nbins:].astype(F32)
    turned = jnp.concatenate(
        [real_part * cosine + imag_part * sine_part, imag_part * cosine - real_part * sine_part],
        axis=-1,
    )
    return turned.astype(BF16)


def pair_products(row_spectra, column_spectra, bin_ids, length):
    results = []
    for lag_index in range(LAGS):
        lag_shift = (lag_index - LAGS // 2) * LAG_STEP
        rotated = rotate(row_spectra, bin_ids, lag_shift, length)
        results.append(
            jnp.einsum("wpk,wqk->pq", rotated, column_spectra, preferred_element_type=F32)
        )
    return jnp.stack(results)


def local_plain(traces, quality_mask, band_bins):
    nbins = band_bins.shape[0]
    windows_here = traces.shape[0]
    samples_here = traces.shape[2]
    sample_times = lax.axis_index("row") * samples_here + jnp.arange(samples_here, dtype=jnp.int32)
    table = band_table(sample_times, band_bins, W)
    partial_value = jnp.einsum("wct,tk->wck", traces, table, preferred_element_type=F32)
    spectra_all = lax.psum(partial_value, "row")
    column_spectra = whiten(spectra_all, quality_mask)
    local_channels = traces.shape[1] // lax.axis_size("row")
    white = lax.dynamic_slice_in_dim(
        column_spectra, lax.axis_index("row") * local_channels, local_channels, 1
    )
    row_spectra = lax.all_gather(white, "col", axis=1, tiled=True)
    scale = 1.0 / math.sqrt(lax.axis_size("sub") * windows_here * nbins)
    partial_products = pair_products(row_spectra, column_spectra, band_bins, W)
    summed = lax.psum_scatter(partial_products, "sub", scatter_dimension=2, tiled=True)
    return summed * scale


def fill_table(first_sample, bins_ref, table_ref, coarse_ref, halfway):
    nbins = bins_ref.shape[1]
    runs = table_ref.shape[0] // FINE
    bins = bins_ref[...]

    def turn(ids, times):
        phase = (ids * times) & (W - 1)
        quarter = (phase + W // 8) // (W // 4)
        angle = (TWO_PI / W) * (phase - quarter * (W // 4)).astype(F32)
        square = angle * angle
        sine = jnp.full_like(square, 1.0 / 362880)
        for term in (-1.0 / 5040, 1.0 / 120, -1.0 / 6, 1.0):
            sine = sine * square + term
        sine = sine * angle
        cosine = jnp.full_like(square, -1.0 / 3628800)
        for term in (1.0 / 40320, -1.0 / 720, 1.0 / 24, -0.5, 1.0):
            cosine = cosine * square + term
        odd = (quarter & 1) == 1
        cosine, sine = jnp.where(odd, sine, cosine), jnp.where(odd, cosine, sine)
        cosine = jnp.where(((quarter + 1) & 2) == 2, -cosine, cosine)
        sine = jnp.where((quarter & 2) == 2, -sine, sine)
        return cosine, sine

    fine_times = lax.broadcasted_iota(jnp.int32, (FINE, nbins), 0)
    coarse_times = first_sample + FINE * lax.broadcasted_iota(jnp.int32, (runs, nbins), 0)
    cos_f, sin_f = turn(bins, fine_times)
    cos_h, sin_h = turn(1, fine_times)
    for place, value in enumerate(turn(bins, coarse_times) + turn(1, coarse_times)):
        coarse_ref[place] = value

    def fill(a):
        cos_c, sin_c, cos_g, sin_g = (coarse_ref[i, pl.ds(a, 1), :] for i in range(4))
        taper = 0.5 - 0.5 * (cos_g * cos_h - sin_g * sin_h)
        rows = pl.ds(pl.multiple_of(a * FINE, FINE), FINE)
        table_ref[rows, :nbins] = (taper * (cos_c * cos_f - sin_c * sin_f)).astype(BF16)
        table_ref[rows, nbins:] = (-taper * (sin_c * cos_f + cos_c * sin_f)).astype(BF16)

    pl.loop(0, runs // 2)(fill)
    halfway()
    pl.loop(runs // 2, runs)(fill)


def spectra_kernel(with_table, firsts, sizes, block, where_ref, bins_or_table, traces_ref, *rest):
    sides = len(sizes)
    outs, bufs, sems = rest[:sides], rest[-sides - 1 : -1], rest[-1]
    windows = traces_ref.shape[0]
    copies = []
    for w in range(windows):
        for i, size in enumerate(sizes):
            start = pl.multiple_of(where_ref[1 + i] * block + firsts[i], 128)
            copies.append(
                pltpu.make_async_copy(
                    traces_ref.at[w, pl.ds(start, size), :], bufs[i].at[w], sems.at[i, w]
                )
            )
    copies[0].start()
    if with_table:
        table_ref, coarse_ref = rest[sides : sides + 2]
        fill_table(where_ref[0], bins_or_table, table_ref, coarse_ref, copies[1].start)
    else:
        table_ref = bins_or_table
        copies[1].start()
    width = table_ref.shape[1]
    for index, copy in enumerate(copies):
        w, i = divmod(index, sides)
        copy.wait()
        if index + 2 < len(copies):
            copies[index + 2].start()
        outs[i][:, w * width : (w + 1) * width] = jnp.dot(
            bufs[i][w], table_ref[...], preferred_element_type=F32
        ).astype(outs[i].dtype)


def spectra_call(where, bins_or_table, traces, firsts, sizes, block, with_table, dtype):
    windows, _, samples = traces.shape
    nbins = bins_or_table.shape[1] if with_table else bins_or_table.shape[1] // 2
    lanes = windows * 2 * nbins
    vmem = pl.BlockSpec(memory_space=pltpu.VMEM)
    out_shape = [jax.ShapeDtypeStruct((size, lanes), dtype) for size in sizes]
    scratch = []
    if with_table:
        out_shape.append(jax.ShapeDtypeStruct((samples, 2 * nbins), BF16))
        scratch.append(pltpu.VMEM((4, samples // FINE, nbins), F32))
    scratch += [pltpu.VMEM((windows, size, samples), BF16) for size in sizes]
    scratch.append(pltpu.SemaphoreType.DMA((len(sizes), windows)))
    return pl.pallas_call(
        functools.partial(spectra_kernel, with_table, firsts, sizes, block),
        out_shape=out_shape,
        in_specs=[
            pl.BlockSpec(memory_space=pltpu.SMEM),
            vmem,
            pl.BlockSpec(memory_space=pl.ANY),
        ],
        out_specs=[vmem] * len(out_shape),
        scratch_shapes=scratch,
        compiler_params=pltpu.CompilerParams(vmem_limit_bytes=SPECTRA_VMEM),
        cost_estimate=SMALL,
        name="spectra",
    )(where, bins_or_table, traces)


def whiten_kernel(got, own, quality, white):
    nbins = got.shape[1] // 4
    mask = quality[...]
    for w in range(2):
        low = w * 2 * nbins
        high = low + nbins
        real = got[:, low : low + nbins].astype(F32) + own[:, low : low + nbins]
        imag = got[:, high : high + nbins].astype(F32) + own[:, high : high + nbins]
        power = real * real + imag * imag
        mean = jnp.sum(power, axis=1, keepdims=True) * (0.5 / nbins)
        factor = mask * jnp.minimum(lax.rsqrt(power), 4.0 * lax.rsqrt(mean + 1e-05))
        white[:, low : low + nbins] = (real * factor).astype(BF16)
        white[:, high : high + nbins] = (imag * factor).astype(BF16)


def whiten_call(got, own, quality):
    vmem = pl.BlockSpec(memory_space=pltpu.VMEM)
    return pl.pallas_call(
        whiten_kernel,
        out_shape=jax.ShapeDtypeStruct(got.shape, BF16),
        in_specs=[vmem] * 3,
        out_specs=vmem,
        compiler_params=pltpu.CompilerParams(vmem_limit_bytes=SMALL_VMEM),
        cost_estimate=SMALL,
        name="whiten",
    )(got, own, quality)


def place_tile(tiles, sems, out, index, sides, start):
    block, width = tiles.shape[1:]
    slot = index % 2
    first = pl.multiple_of(sides[index // LAGS] * block, 128)
    return pltpu.make_async_copy(
        tiles.at[slot],
        out.at[index % LAGS, pl.ds(first, block), pl.ds(start, width)],
        sems.at[slot],
    )


def times_columns(scale, rows, columns):
    return scale * lax.dot_general(
        rows, columns, (((1,), (1,)), ((), ())), preferred_element_type=F32
    )


def first_kernel(gather, scale, count, info, cos_ref, sin_ref, *refs):
    whites = refs[:4]
    parts = refs[4 : 4 + count]
    out, rows_out, columns, turned, tiles, sems, row_sems = refs[4 + count :]
    nbins = cos_ref.shape[1]
    half = whites[0].shape[1]
    start = pl.multiple_of(info[2], 128)
    gather(info, parts, columns)
    steps = 2 * LAGS

    def place(index):
        return place_tile(tiles, sems, out, index, info, start)

    def keep(index):
        slot = lax.rem(index, 2)
        return pltpu.make_async_copy(turned.at[slot], rows_out.at[index], row_sems.at[slot])

    for side in range(2):

        @pl.loop(side * LAGS, (side + 1) * LAGS)
        def _(step):
            slot = lax.rem(step, 2)

            @pl.when(step >= 2)
            def _():
                place(step - 2).wait()
                keep(step - 2).wait()

            lag = lax.rem(step, LAGS)
            cosine = cos_ref[pl.ds(lag, 1), :]
            sine = sin_ref[pl.ds(lag, 1), :]
            for part in range(2):
                ref = whites[2 * side + part]
                for w in range(2):
                    low = w * 2 * nbins
                    high = low + nbins
                    real = ref[:, low : low + nbins].astype(F32)
                    imag = ref[:, high : high + nbins].astype(F32)
                    base = part * half
                    turned[slot, :, base + low : base + low + nbins] = (
                        real * cosine + imag * sine
                    ).astype(BF16)
                    turned[slot, :, base + high : base + high + nbins] = (
                        imag * cosine - real * sine
                    ).astype(BF16)
            keep(step).start()
            tiles[slot] = times_columns(scale, turned[slot], columns[...])
            place(step).start()

    for step in (steps - 2, steps - 1):
        place(step).wait()
        keep(step).wait()


def first_call(info, cosine, sine, whites, parts, gather, width, scale, out_shape):
    block, half = whites[0].shape
    vmem = pl.BlockSpec(memory_space=pltpu.VMEM)
    hbm = pl.BlockSpec(memory_space=pltpu.HBM)
    return pl.pallas_call(
        functools.partial(first_kernel, gather, scale, len(parts)),
        out_shape=[out_shape, jax.ShapeDtypeStruct((ROWS_KEPT, block, 2 * half), BF16)],
        in_specs=[pl.BlockSpec(memory_space=pltpu.SMEM)] + [vmem] * (6 + len(parts)),
        out_specs=[hbm, hbm],
        scratch_shapes=[
            pltpu.VMEM((width, 2 * half), BF16),
            pltpu.VMEM((2, block, 2 * half), BF16),
            pltpu.VMEM((2, block, width), F32),
            pltpu.SemaphoreType.DMA((2,)),
            pltpu.SemaphoreType.DMA((2,)),
        ],
        compiler_params=pltpu.CompilerParams(vmem_limit_bytes=PRODUCT_VMEM),
        cost_estimate=SMALL,
        name="turn_products",
    )(info, cosine, sine, *whites, *parts)


def product_kernel(gather, scale, fetch, count, *refs):
    info, rows = refs[:2]
    parts = refs[2 : 2 + count]
    out = refs[3 + count]
    steps = 2 * LAGS
    start = pl.multiple_of(info[2], 128)
    if fetch:
        held, columns, tiles, sems, fetch_sems = refs[4 + count :]
    else:
        columns, tiles, sems = refs[4 + count :]
        held = rows

    def place(index):
        return place_tile(tiles, sems, out, index, info, start)

    def bring(index):
        return pltpu.make_async_copy(rows.at[index], held.at[index], fetch_sems.at[index])

    if fetch:
        for step in range(AHEAD):
            bring(step).start()
    gather(info, parts, columns)

    def run(step):
        if fetch:

            @pl.when(step + AHEAD < steps)
            def _():
                bring(step + AHEAD).start()

            bring(step).wait()

        @pl.when(step >= 2)
        def _():
            place(step - 2).wait()

        tiles[lax.rem(step, 2)] = times_columns(scale, held[step], columns[...])
        place(step).start()

    if fetch:
        pl.loop(0, steps)(run)
    else:
        for step in range(steps):
            if step >= 2:
                place(step - 2).wait()
            tiles[step % 2] = times_columns(scale, held[step], columns[...])
            place(step).start()
    place(steps - 2).wait()
    place(steps - 1).wait()


def product_call(info, rows, parts, gather, width, scale, base, fetch):
    _, block, depth = rows.shape
    vmem = pl.BlockSpec(memory_space=pltpu.VMEM)
    hbm = pl.BlockSpec(memory_space=pltpu.HBM)
    out_shape = [jax.ShapeDtypeStruct(base.shape, base.dtype)]
    out_specs = [hbm]
    scratch = [
        pltpu.VMEM((width, depth), BF16),
        pltpu.VMEM((2, block, width), F32),
        pltpu.SemaphoreType.DMA((2,)),
    ]
    if fetch:
        out_shape.append(jax.ShapeDtypeStruct((2 * LAGS, block, depth), rows.dtype))
        out_specs.append(vmem)
        scratch.append(pltpu.SemaphoreType.DMA((2 * LAGS,)))
    return pl.pallas_call(
        functools.partial(product_kernel, gather, scale, fetch, len(parts)),
        out_shape=out_shape,
        in_specs=[pl.BlockSpec(memory_space=pltpu.SMEM), hbm if fetch else vmem]
        + [vmem] * len(parts)
        + [hbm],
        out_specs=out_specs,
        scratch_shapes=scratch,
        input_output_aliases={2 + len(parts): 0},
        compiler_params=pltpu.CompilerParams(vmem_limit_bytes=PRODUCT_VMEM),
        cost_estimate=SMALL,
        name="products",
    )(info, rows, *parts, base)


def put(columns, first, rows, own, other):
    half = own.shape[1]
    count = rows.stop - rows.start
    columns[first : first + count, :half] = own[rows, :]
    columns[first : first + count, half:] = other[rows, :]


def gather_full(info, parts, columns):
    own_o, own_t, right_o, right_t, left_o, left_t = parts
    split = right_o.shape[0]

    @pl.when(info[3] == 1)
    def _():
        put(columns, 0, slice(0, own_o.shape[0]), own_o, own_t)

    @pl.when(info[3] == 0)
    def _():
        put(columns, 0, slice(0, split), right_o, right_t)
        put(columns, split, slice(0, left_o.shape[0]), left_o, left_t)


def gather_first(info, parts, columns):
    right_o, right_t, left_o, left_t = parts
    rows = slice(0, columns.shape[0])

    @pl.when(info[3] == 1)
    def _():
        put(columns, 0, rows, right_o, right_t)

    @pl.when(info[3] == 0)
    def _():
        put(columns, 0, rows, left_o, left_t)


def gather_last(info, parts, columns):
    early_o, early_t, right_o, right_t, left_o, left_t = parts
    split, rest = right_o.shape[0], left_o.shape[0]

    @pl.when(info[3] == 1)
    def _():
        put(columns, 0, slice(rest, split), early_o, early_t)
        put(columns, split - rest, slice(0, rest), left_o, left_t)

    @pl.when(info[3] == 0)
    def _():
        put(columns, 0, slice(0, split), right_o, right_t)


def local_rings(traces, quality_mask, band_bins):
    n = lax.axis_size("row")
    windows, channels, samples = traces.shape
    nbins = band_bins.shape[0]
    block = channels // n
    split = (block // 128 + 1) // 2 * 128
    rest = block - split
    z = lax.axis_index("row")
    x = lax.axis_index("col")
    c = lax.axis_index("sub")
    to_right = [(i, (i + 1) % n) for i in range(n)]
    to_left = [(i, (i - 1) % n) for i in range(n)]
    i32 = jnp.int32

    def where(*blocks):
        return jnp.stack([z * samples, *(b % n for b in blocks)]).astype(i32)

    right, left, table = spectra_call(
        where(z - 1, z + 1), band_bins[None, :], traces, (0, split), (split, rest), block, True, BF16
    )
    for k in range(1, n):
        places = where(z - 1 - k, z + 1 + k)
        if k > 1:
            places = lax.optimization_barrier((places, right, left))[0]
        own_r, own_l = spectra_call(
            places, table, traces, (0, split), (split, rest), block, False, F32
        )
        right = lax.ppermute(right, "row", to_right)
        left = lax.ppermute(left, "row", to_left)
        if k < n - 1:
            right = (right.astype(F32) + own_r).astype(BF16)
            left = (left.astype(F32) + own_l).astype(BF16)
    quality = lax.dynamic_slice_in_dim(quality_mask, z * block, block).astype(F32)[:, None]
    right = whiten_call(right, own_r, quality[:split])
    left = whiten_call(left, own_l, quality[split:])
    white = jnp.concatenate([right, left], axis=0)

    def pairs(step, move, cross):
        found = []
        for i in range(n):
            core = (i - step * move) % n * 2 // n
            source = 1 - core if cross else core
            found.append((i * 2 + source, (i + move) % n * 2 + core))
        return found

    def last_step(part, move):
        return [lax.ppermute(part, axes, pairs(n - 2, move, cross)) for cross in (False, True)]

    axes = ("row", "sub")
    swap = [(0, 1), (1, 0)]
    right0 = lax.ppermute(right, "row", to_right)
    left0 = lax.ppermute(left, "row", to_left)
    white_t = lax.ppermute(white, "sub", swap)
    far = lax.ppermute(white, "col", swap)
    right1 = lax.ppermute(right0, "row", to_right)
    left1 = lax.ppermute(left0, "row", to_left)
    r0 = [right0, lax.ppermute(right0, "sub", swap)]
    l0 = [left0, lax.ppermute(left0, "sub", swap)]
    far_t = lax.ppermute(far, "sub", swap)

    shifts = jnp.array([(lag - LAGS // 2) * LAG_STEP for lag in range(LAGS)], i32)
    angles = TWO_PI / W * (band_bins[None, :] * shifts[:, None] % W).astype(F32)
    cosine, sine = jnp.cos(angles), jnp.sin(angles)
    per_core = n // 2
    owner = z // per_core == c
    from_right = (z - 1) % n // per_core == c
    full = jnp.where(owner, z, (z + 2) % n) - per_core * c
    other = 1 - full
    scale = 1.0 / math.sqrt(2 * windows * nbins)
    out_shape = jax.ShapeDtypeStruct((LAGS, 2 * block, per_core * block), F32)
    first_start = other * block + jnp.where(from_right, 0, split)
    last_start = other * block + jnp.where(from_right, rest, 0)

    def info(start, flag):
        return jnp.stack([x, 1 - x, start, flag]).astype(i32)

    result, rows = first_call(
        info(first_start, from_right), cosine, sine, [white, white_t, far, far_t], r0 + l0,
        gather_first, rest, scale, out_shape,
    )
    right1 = lax.optimization_barrier((right1, result))[0]
    left1 = lax.optimization_barrier((left1, result))[0]
    r2 = last_step(right1, 1)
    l2 = last_step(left1, -1)
    r1 = [right1, lax.ppermute(right1, "sub", swap)]
    l1 = [left1, lax.ppermute(left1, "sub", swap)]
    result, rows = product_call(
        info(full * block, owner), rows, [white, white_t] + r1 + l1,
        gather_full, block, scale, result, True,
    )
    return product_call(
        info(last_start, from_right), rows, r0 + r2 + l2,
        gather_last, split, scale, result, False,
    )[0]


def solution(mesh):
    in_specs = (P(("group", "sub"), "col", "row"), P("col"), P())
    out_specs = P("group", "row", ("col", "sub"))
    rings = (mesh.shape["row"], mesh.shape["col"], mesh.shape["sub"]) == (4, 2, 2)
    return jax.shard_map(
        local_rings if rings else local_plain,
        mesh=mesh, in_specs=in_specs, out_specs=out_specs, check_vma=False,
    )
```

```python
import functools
import math

import jax
import jax.numpy as jnp
from jax import lax
from jax.experimental import pallas as pl
from jax.experimental.pallas import tpu as pltpu
from jax.sharding import PartitionSpec as P

W = 16384
LAGS = 4
LAG_STEP = 50
TWO_PI = 2.0 * math.pi

F32 = jnp.float32
BF16 = jnp.bfloat16
MIB = 1024 * 1024
SPECTRA_VMEM = 18 * MIB
SMALL_VMEM = 8 * MIB
PRODUCT_VMEM = 16 * MIB
SMALL = pl.CostEstimate(flops=1000, bytes_accessed=1000, transcendentals=0)
AHEAD = 3
ROWS_KEPT = 48
FINE = 64


def band_table(sample_times, bin_ids, length):
    window_taper = 0.5 - 0.5 * jnp.cos(TWO_PI / length * sample_times.astype(F32))
    phase_index = sample_times[:, None] * bin_ids[None, :] % length
    angles = TWO_PI / length * phase_index.astype(F32)
    cosine = window_taper[:, None] * jnp.cos(angles)
    sine_part = -window_taper[:, None] * jnp.sin(angles)
    return jnp.concatenate([cosine, sine_part], axis=1).astype(BF16)


def whiten(spectra, quality):
    nbins = spectra.shape[-1] // 2
    real_part = spectra[..., :nbins]
    imag_part = spectra[..., nbins:]
    band_rms = jnp.sqrt(jnp.mean(spectra * spectra, axis=-1, keepdims=True) + 1e-05)
    magnitude = jnp.sqrt(real_part * real_part + imag_part * imag_part)
    divisor = jnp.maximum(magnitude, 0.25 * band_rms)
    scaled = jnp.concatenate([real_part / divisor, imag_part / divisor], axis=-1)
    return (quality.astype(F32)[:, None] * scaled).astype(BF16)


def rotate(white, bin_ids, lag_shift, length):
    nbins = white.shape[-1] // 2
    phase_index = bin_ids * lag_shift % length
    angles = TWO_PI / length * phase_index.astype(F32)
    cosine = jnp.cos(angles)
    sine_part = jnp.sin(angles)
    real_part = white[..., :nbins].astype(F32)
    imag_part = white[..., nbins:].astype(F32)
    turned = jnp.concatenate(
        [real_part * cosine + imag_part * sine_part, imag_part * cosine - real_part * sine_part],
        axis=-1,
    )
    return turned.astype(BF16)


def pair_products(row_spectra, column_spectra, bin_ids, length):
    results = []
    for lag_index in range(LAGS):
        lag_shift = (lag_index - LAGS // 2) * LAG_STEP
        rotated = rotate(row_spectra, bin_ids, lag_shift, length)
        results.append(
            jnp.einsum("wpk,wqk->pq", rotated, column_spectra, preferred_element_type=F32)
        )
    return jnp.stack(results)


def local_plain(traces, quality_mask, band_bins):
    nbins = band_bins.shape[0]
    windows_here = traces.shape[0]
    samples_here = traces.shape[2]
    sample_times = lax.axis_index("row") * samples_here + jnp.arange(samples_here, dtype=jnp.int32)
    table = band_table(sample_times, band_bins, W)
    partial_value = jnp.einsum("wct,tk->wck", traces, table, preferred_element_type=F32)
    spectra_all = lax.psum(partial_value, "row")
    column_spectra = whiten(spectra_all, quality_mask)
    local_channels = traces.shape[1] // lax.axis_size("row")
    white = lax.dynamic_slice_in_dim(
        column_spectra, lax.axis_index("row") * local_channels, local_channels, 1
    )
    row_spectra = lax.all_gather(white, "col", axis=1, tiled=True)
    scale = 1.0 / math.sqrt(lax.axis_size("sub") * windows_here * nbins)
    partial_products = pair_products(row_spectra, column_spectra, band_bins, W)
    summed = lax.psum_scatter(partial_products, "sub", scatter_dimension=2, tiled=True)
    return summed * scale


def fill_table(first_sample, bins_ref, table_ref, coarse_ref, halfway):
    nbins = bins_ref.shape[1]
    runs = table_ref.shape[0] // FINE
    bins = bins_ref[...]

    def turn(ids, times):
        phase = (ids * times) & (W - 1)
        quarter = (phase + W // 8) // (W // 4)
        angle = (TWO_PI / W) * (phase - quarter * (W // 4)).astype(F32)
        square = angle * angle
        sine = jnp.full_like(square, 1.0 / 362880)
        for term in (-1.0 / 5040, 1.0 / 120, -1.0 / 6, 1.0):
            sine = sine * square + term
        sine = sine * angle
        cosine = jnp.full_like(square, -1.0 / 3628800)
        for term in (1.0 / 40320, -1.0 / 720, 1.0 / 24, -0.5, 1.0):
            cosine = cosine * square + term
        odd = (quarter & 1) == 1
        cosine, sine = jnp.where(odd, sine, cosine), jnp.where(odd, cosine, sine)
        cosine = jnp.where(((quarter + 1) & 2) == 2, -cosine, cosine)
        sine = jnp.where((quarter & 2) == 2, -sine, sine)
        return cosine, sine

    fine_times = lax.broadcasted_iota(jnp.int32, (FINE, nbins), 0)
    coarse_times = first_sample + FINE * lax.broadcasted_iota(jnp.int32, (runs, nbins), 0)
    cos_f, sin_f = turn(bins, fine_times)
    cos_h, sin_h = turn(1, fine_times)
    for place, value in enumerate(turn(bins, coarse_times) + turn(1, coarse_times)):
        coarse_ref[place] = value

    def fill(a):
        cos_c, sin_c, cos_g, sin_g = (coarse_ref[i, pl.ds(a, 1), :] for i in range(4))
        taper = 0.5 - 0.5 * (cos_g * cos_h - sin_g * sin_h)
        rows = pl.ds(pl.multiple_of(a * FINE, FINE), FINE)
        table_ref[rows, :nbins] = (taper * (cos_c * cos_f - sin_c * sin_f)).astype(BF16)
        table_ref[rows, nbins:] = (-taper * (sin_c * cos_f + cos_c * sin_f)).astype(BF16)

    pl.loop(0, runs // 2)(fill)
    halfway()
    pl.loop(runs // 2, runs)(fill)


def spectra_kernel(with_table, firsts, sizes, block, where_ref, bins_or_table, traces_ref, *rest):
    sides = len(sizes)
    outs, bufs, sems = rest[:sides], rest[-sides - 1 : -1], rest[-1]
    windows = traces_ref.shape[0]
    copies = []
    for w in range(windows):
        for i, size in enumerate(sizes):
            start = pl.multiple_of(where_ref[1 + i] * block + firsts[i], 128)
            copies.append(
                pltpu.make_async_copy(
                    traces_ref.at[w, pl.ds(start, size), :], bufs[i].at[w], sems.at[i, w]
                )
            )
    copies[0].start()
    if with_table:
        table_ref, coarse_ref = rest[sides : sides + 2]
        fill_table(where_ref[0], bins_or_table, table_ref, coarse_ref, copies[1].start)
    else:
        table_ref = bins_or_table
        copies[1].start()
    width = table_ref.shape[1]
    for index, copy in enumerate(copies):
        w, i = divmod(index, sides)
        copy.wait()
        if index + 2 < len(copies):
            copies[index + 2].start()
        outs[i][:, w * width : (w + 1) * width] = jnp.dot(
            bufs[i][w], table_ref[...], preferred_element_type=F32
        ).astype(outs[i].dtype)


def spectra_call(where, bins_or_table, traces, firsts, sizes, block, with_table, dtype):
    windows, _, samples = traces.shape
    nbins = bins_or_table.shape[1] if with_table else bins_or_table.shape[1] // 2
    lanes = windows * 2 * nbins
    vmem = pl.BlockSpec(memory_space=pltpu.VMEM)
    out_shape = [jax.ShapeDtypeStruct((size, lanes), dtype) for size in sizes]
    scratch = []
    if with_table:
        out_shape.append(jax.ShapeDtypeStruct((samples, 2 * nbins), BF16))
        scratch.append(pltpu.VMEM((4, samples // FINE, nbins), F32))
    scratch += [pltpu.VMEM((windows, size, samples), BF16) for size in sizes]
    scratch.append(pltpu.SemaphoreType.DMA((len(sizes), windows)))
    return pl.pallas_call(
        functools.partial(spectra_kernel, with_table, firsts, sizes, block),
        out_shape=out_shape,
        in_specs=[
            pl.BlockSpec(memory_space=pltpu.SMEM),
            vmem,
            pl.BlockSpec(memory_space=pl.ANY),
        ],
        out_specs=[vmem] * len(out_shape),
        scratch_shapes=scratch,
        compiler_params=pltpu.CompilerParams(vmem_limit_bytes=SPECTRA_VMEM),
        cost_estimate=SMALL,
        name="spectra",
    )(where, bins_or_table, traces)


def whiten_kernel(got, own, quality, white):
    nbins = got.shape[1] // 4
    mask = quality[...]
    for w in range(2):
        low = w * 2 * nbins
        high = low + nbins
        real = got[:, low : low + nbins].astype(F32) + own[:, low : low + nbins]
        imag = got[:, high : high + nbins].astype(F32) + own[:, high : high + nbins]
        power = real * real + imag * imag
        mean = jnp.sum(power, axis=1, keepdims=True) * (0.5 / nbins)
        factor = mask * jnp.minimum(lax.rsqrt(power), 4.0 * lax.rsqrt(mean + 1e-05))
        white[:, low : low + nbins] = (real * factor).astype(BF16)
        white[:, high : high + nbins] = (imag * factor).astype(BF16)


def whiten_call(got, own, quality):
    vmem = pl.BlockSpec(memory_space=pltpu.VMEM)
    return pl.pallas_call(
        whiten_kernel,
        out_shape=jax.ShapeDtypeStruct(got.shape, BF16),
        in_specs=[vmem] * 3,
        out_specs=vmem,
        compiler_params=pltpu.CompilerParams(vmem_limit_bytes=SMALL_VMEM),
        cost_estimate=SMALL,
        name="whiten",
    )(got, own, quality)


def place_tile(tiles, sems, out, index, sides, starts):
    block = tiles.shape[1]
    slot = index % 2
    first = pl.multiple_of(sides[index // LAGS] * block, 128)
    return [
        pltpu.make_async_copy(
            tiles.at[slot, :, pl.ds(low, lanes)],
            out.at[index % LAGS, pl.ds(first, block), pl.ds(pl.multiple_of(start, 128), lanes)],
            sems.at[slot, i],
        )
        for i, (low, lanes, start) in enumerate(starts)
    ]


def times_columns(scale, rows, columns):
    return scale * lax.dot_general(
        rows, columns, (((1,), (1,)), ((), ())), preferred_element_type=F32
    )


def first_kernel(gather, scale, count, info, cos_ref, sin_ref, *refs):
    whites = refs[:4]
    parts = refs[4 : 4 + count]
    out, rows_out, columns, turned, tiles, sems, row_sems = refs[4 + count :]
    nbins = cos_ref.shape[1]
    half = whites[0].shape[1]
    gather(info, parts, columns)
    steps = 2 * LAGS

    def place(index):
        return place_tile(tiles, sems, out, index, info, [(0, tiles.shape[2], info[2])])[0]

    def keep(index):
        slot = lax.rem(index, 2)
        return pltpu.make_async_copy(turned.at[slot], rows_out.at[index], row_sems.at[slot])

    for side in range(2):

        @pl.loop(side * LAGS, (side + 1) * LAGS)
        def _(step):
            slot = lax.rem(step, 2)

            @pl.when(step >= 2)
            def _():
                place(step - 2).wait()
                keep(step - 2).wait()

            lag = lax.rem(step, LAGS)
            cosine = cos_ref[pl.ds(lag, 1), :]
            sine = sin_ref[pl.ds(lag, 1), :]
            for part in range(2):
                ref = whites[2 * side + part]
                for w in range(2):
                    low = w * 2 * nbins
                    high = low + nbins
                    real = ref[:, low : low + nbins].astype(F32)
                    imag = ref[:, high : high + nbins].astype(F32)
                    base = part * half
                    turned[slot, :, base + low : base + low + nbins] = (
                        real * cosine + imag * sine
                    ).astype(BF16)
                    turned[slot, :, base + high : base + high + nbins] = (
                        imag * cosine - real * sine
                    ).astype(BF16)
            keep(step).start()
            tiles[slot] = times_columns(scale, turned[slot], columns[...])
            place(step).start()

    for step in (steps - 2, steps - 1):
        place(step).wait()
        keep(step).wait()


def first_call(info, cosine, sine, whites, parts, gather, width, scale, out_shape):
    block, half = whites[0].shape
    vmem = pl.BlockSpec(memory_space=pltpu.VMEM)
    hbm = pl.BlockSpec(memory_space=pltpu.HBM)
    return pl.pallas_call(
        functools.partial(first_kernel, gather, scale, len(parts)),
        out_shape=[out_shape, jax.ShapeDtypeStruct((ROWS_KEPT, block, 2 * half), BF16)],
        in_specs=[pl.BlockSpec(memory_space=pltpu.SMEM)] + [vmem] * (6 + len(parts)),
        out_specs=[hbm, hbm],
        scratch_shapes=[
            pltpu.VMEM((width, 2 * half), BF16),
            pltpu.VMEM((2, block, 2 * half), BF16),
            pltpu.VMEM((2, block, width), F32),
            pltpu.SemaphoreType.DMA((2, 1)),
            pltpu.SemaphoreType.DMA((2,)),
        ],
        compiler_params=pltpu.CompilerParams(vmem_limit_bytes=PRODUCT_VMEM),
        cost_estimate=SMALL,
        name="turn_products",
    )(info, cosine, sine, *whites, *parts)


def product_kernel(gather, widths, scale, fetch, count, *refs):
    info, rows = refs[:2]
    parts = refs[2 : 2 + count]
    out = refs[3 + count]
    steps = 2 * LAGS
    if fetch:
        held, columns, tiles, sems, fetch_sems = refs[4 + count :]
    else:
        columns, tiles, sems = refs[4 + count :]
        held = rows

    lows = [sum(widths[:i]) for i in range(len(widths))]
    starts = [(lows[i], widths[i], info[2 + 2 * i]) for i in range(len(widths))]

    def start_placing(index):
        for copy in place_tile(tiles, sems, out, index, info, starts):
            copy.start()

    def end_placing(index):
        for copy in place_tile(tiles, sems, out, index, info, starts):
            copy.wait()

    def bring(index):
        return pltpu.make_async_copy(rows.at[index], held.at[index], fetch_sems.at[index])

    if fetch:
        for step in range(AHEAD):
            bring(step).start()
    gather(info, parts, columns)

    def run(step):
        if fetch:

            @pl.when(step + AHEAD < steps)
            def _():
                bring(step + AHEAD).start()

            bring(step).wait()

        @pl.when(step >= 2)
        def _():
            end_placing(step - 2)

        tiles[lax.rem(step, 2)] = times_columns(scale, held[step], columns[...])
        start_placing(step)

    if fetch:
        pl.loop(0, steps)(run)
    else:
        for step in range(steps):
            if step >= 2:
                end_placing(step - 2)
            tiles[step % 2] = times_columns(scale, held[step], columns[...])
            start_placing(step)
    end_placing(steps - 2)
    end_placing(steps - 1)


def product_call(info, rows, parts, gather, widths, scale, base, fetch):
    _, block, depth = rows.shape
    width = sum(widths)
    vmem = pl.BlockSpec(memory_space=pltpu.VMEM)
    hbm = pl.BlockSpec(memory_space=pltpu.HBM)
    out_shape = [jax.ShapeDtypeStruct(base.shape, base.dtype)]
    out_specs = [hbm]
    scratch = [
        pltpu.VMEM((width, depth), BF16),
        pltpu.VMEM((2, block, width), F32),
        pltpu.SemaphoreType.DMA((2, len(widths))),
    ]
    if fetch:
        out_shape.append(jax.ShapeDtypeStruct((2 * LAGS, block, depth), rows.dtype))
        out_specs.append(vmem)
        scratch.append(pltpu.SemaphoreType.DMA((2 * LAGS,)))
    return pl.pallas_call(
        functools.partial(product_kernel, gather, widths, scale, fetch, len(parts)),
        out_shape=out_shape,
        in_specs=[pl.BlockSpec(memory_space=pltpu.SMEM), hbm if fetch else vmem]
        + [vmem] * len(parts)
        + [hbm],
        out_specs=out_specs,
        scratch_shapes=scratch,
        input_output_aliases={2 + len(parts): 0},
        compiler_params=pltpu.CompilerParams(vmem_limit_bytes=PRODUCT_VMEM),
        cost_estimate=SMALL,
        name="products",
    )(info, rows, *parts, base)


def put(columns, first, rows, own, other):
    half = own.shape[1]
    count = rows.stop - rows.start
    columns[first : first + count, :half] = own[rows, :]
    columns[first : first + count, half:] = other[rows, :]


def gather_full(info, parts, columns):
    own_o, own_t, right_o, right_t, left_o, left_t = parts
    split, count = right_o.shape[0], columns.shape[0]

    @pl.when(info[3] == 1)
    def _():
        put(columns, 0, slice(0, count), own_o, own_t)

    @pl.when(info[3] == 0)
    def _():
        put(columns, 0, slice(0, split), right_o, right_t)
        put(columns, split, slice(0, count - split), left_o, left_t)


def gather_first(info, parts, columns):
    right_o, right_t, left_o, left_t = parts
    rows = slice(0, columns.shape[0])

    @pl.when(info[3] == 1)
    def _():
        put(columns, 0, rows, right_o, right_t)

    @pl.when(info[3] == 0)
    def _():
        put(columns, 0, rows, left_o, left_t)


def gather_last(info, parts, columns):
    early_o, early_t, right_o, right_t, left_o, left_t, own_o, own_t, tail_o, tail_t = parts
    split, rest = right_o.shape[0], left_o.shape[0]
    tail = columns.shape[0] - split

    @pl.when(info[3] == 1)
    def _():
        put(columns, 0, slice(rest, split), early_o, early_t)
        put(columns, split - rest, slice(0, rest), left_o, left_t)

    @pl.when(info[3] == 0)
    def _():
        put(columns, 0, slice(0, split), right_o, right_t)

    @pl.when(info[5] == 1)
    def _():
        put(columns, split, slice(own_o.shape[0] - tail, own_o.shape[0]), own_o, own_t)

    @pl.when(info[5] == 0)
    def _():
        put(columns, split, slice(tail_o.shape[0] - tail, tail_o.shape[0]), tail_o, tail_t)


def local_rings(traces, quality_mask, band_bins):
    n = lax.axis_size("row")
    windows, channels, samples = traces.shape
    nbins = band_bins.shape[0]
    block = channels // n
    split = (block // 128 + 1) // 2 * 128
    rest = block - split
    z = lax.axis_index("row")
    x = lax.axis_index("col")
    c = lax.axis_index("sub")
    to_right = [(i, (i + 1) % n) for i in range(n)]
    to_left = [(i, (i - 1) % n) for i in range(n)]
    i32 = jnp.int32

    def where(*blocks):
        return jnp.stack([z * samples, *(b % n for b in blocks)]).astype(i32)

    right, left, table = spectra_call(
        where(z - 1, z + 1), band_bins[None, :], traces, (0, split), (split, rest), block, True, BF16
    )
    for k in range(1, n):
        places = where(z - 1 - k, z + 1 + k)
        if k > 1:
            places = lax.optimization_barrier((places, right, left))[0]
        own_r, own_l = spectra_call(
            places, table, traces, (0, split), (split, rest), block, False, F32
        )
        right = lax.ppermute(right, "row", to_right)
        left = lax.ppermute(left, "row", to_left)
        if k < n - 1:
            right = (right.astype(F32) + own_r).astype(BF16)
            left = (left.astype(F32) + own_l).astype(BF16)
    quality = lax.dynamic_slice_in_dim(quality_mask, z * block, block).astype(F32)[:, None]
    right = whiten_call(right, own_r, quality[:split])
    left = whiten_call(left, own_l, quality[split:])
    white = jnp.concatenate([right, left], axis=0)

    def pairs(step, move, cross):
        found = []
        for i in range(n):
            core = (i - step * move) % n * 2 // n
            source = 1 - core if cross else core
            found.append((i * 2 + source, (i + move) % n * 2 + core))
        return found

    def last_step(part, move):
        return [lax.ppermute(part, axes, pairs(n - 2, move, cross)) for cross in (False, True)]

    axes = ("row", "sub")
    swap = [(0, 1), (1, 0)]
    right0 = lax.ppermute(right, "row", to_right)
    left0 = lax.ppermute(left, "row", to_left)
    white_t = lax.ppermute(white, "sub", swap)
    far = lax.ppermute(white, "col", swap)
    right1 = lax.ppermute(right0, "row", to_right)
    left1 = lax.ppermute(left0, "row", to_left)
    r0 = [right0, lax.ppermute(right0, "sub", swap)]
    l0 = [left0, lax.ppermute(left0, "sub", swap)]
    far_t = lax.ppermute(far, "sub", swap)

    shifts = jnp.array([(lag - LAGS // 2) * LAG_STEP for lag in range(LAGS)], i32)
    angles = TWO_PI / W * (band_bins[None, :] * shifts[:, None] % W).astype(F32)
    cosine, sine = jnp.cos(angles), jnp.sin(angles)
    tail = 128
    per_core = n // 2
    owner = z // per_core == c
    from_right = (z - 1) % n // per_core == c
    full = jnp.where(owner, z, (z + 2) % n) - per_core * c
    other = 1 - full
    scale = 1.0 / math.sqrt(2 * windows * nbins)
    out_shape = jax.ShapeDtypeStruct((LAGS, 2 * block, per_core * block), F32)
    first_start = other * block + jnp.where(from_right, 0, split)
    last_start = other * block + jnp.where(from_right, rest, 0)

    def info(*places):
        return jnp.stack([x, 1 - x, *places]).astype(i32)

    result, rows = first_call(
        info(first_start, from_right), cosine, sine, [white, white_t, far, far_t], r0 + l0,
        gather_first, rest, scale, out_shape,
    )
    right1 = lax.optimization_barrier((right1, result))[0]
    left1 = lax.optimization_barrier((left1, result))[0]
    r2 = last_step(right1, 1)
    l2 = last_step(left1, -1)
    r1 = [right1, lax.ppermute(right1, "sub", swap)]
    l1 = [left1, lax.ppermute(left1, "sub", swap)]
    result, rows = product_call(
        info(full * block, owner), rows, [white, white_t] + r1 + l1,
        gather_full, (block - tail,), scale, result, True,
    )
    return product_call(
        info(last_start, from_right, full * block + block - tail, owner), rows,
        r0 + r2 + l2 + [white, white_t] + l1, gather_last, (split, tail), scale, result, False,
    )[0]


def solution(mesh):
    in_specs = (P(("group", "sub"), "col", "row"), P("col"), P())
    out_specs = P("group", "row", ("col", "sub"))
    rings = (mesh.shape["row"], mesh.shape["col"], mesh.shape["sub"]) == (4, 2, 2)
    return jax.shard_map(
        local_rings if rings else local_plain,
        mesh=mesh, in_specs=in_specs, out_specs=out_specs, check_vma=False,
    )
```

```python
import functools
import math

import jax
import jax.numpy as jnp
from jax import lax
from jax.experimental import pallas as pl
from jax.experimental.pallas import tpu as pltpu
from jax.sharding import PartitionSpec as P

W = 16384
LAGS = 4
LAG_STEP = 50
TWO_PI = 2.0 * math.pi

F32 = jnp.float32
BF16 = jnp.bfloat16
MIB = 1024 * 1024
SPECTRA_VMEM = 18 * MIB
SMALL_VMEM = 8 * MIB
PRODUCT_VMEM = 16 * MIB
SMALL = pl.CostEstimate(flops=1000, bytes_accessed=1000, transcendentals=0)
TILES = 3
AHEAD = 5
ROWS_KEPT = 48
FINE = 64


def band_table(sample_times, bin_ids, length):
    window_taper = 0.5 - 0.5 * jnp.cos(TWO_PI / length * sample_times.astype(F32))
    phase_index = sample_times[:, None] * bin_ids[None, :] % length
    angles = TWO_PI / length * phase_index.astype(F32)
    cosine = window_taper[:, None] * jnp.cos(angles)
    sine_part = -window_taper[:, None] * jnp.sin(angles)
    return jnp.concatenate([cosine, sine_part], axis=1).astype(BF16)


def whiten(spectra, quality):
    nbins = spectra.shape[-1] // 2
    real_part = spectra[..., :nbins]
    imag_part = spectra[..., nbins:]
    band_rms = jnp.sqrt(jnp.mean(spectra * spectra, axis=-1, keepdims=True) + 1e-05)
    magnitude = jnp.sqrt(real_part * real_part + imag_part * imag_part)
    divisor = jnp.maximum(magnitude, 0.25 * band_rms)
    scaled = jnp.concatenate([real_part / divisor, imag_part / divisor], axis=-1)
    return (quality.astype(F32)[:, None] * scaled).astype(BF16)


def rotate(white, bin_ids, lag_shift, length):
    nbins = white.shape[-1] // 2
    phase_index = bin_ids * lag_shift % length
    angles = TWO_PI / length * phase_index.astype(F32)
    cosine = jnp.cos(angles)
    sine_part = jnp.sin(angles)
    real_part = white[..., :nbins].astype(F32)
    imag_part = white[..., nbins:].astype(F32)
    turned = jnp.concatenate(
        [real_part * cosine + imag_part * sine_part, imag_part * cosine - real_part * sine_part],
        axis=-1,
    )
    return turned.astype(BF16)


def pair_products(row_spectra, column_spectra, bin_ids, length):
    results = []
    for lag_index in range(LAGS):
        lag_shift = (lag_index - LAGS // 2) * LAG_STEP
        rotated = rotate(row_spectra, bin_ids, lag_shift, length)
        results.append(
            jnp.einsum("wpk,wqk->pq", rotated, column_spectra, preferred_element_type=F32)
        )
    return jnp.stack(results)


def local_plain(traces, quality_mask, band_bins):
    nbins = band_bins.shape[0]
    windows_here = traces.shape[0]
    samples_here = traces.shape[2]
    sample_times = lax.axis_index("row") * samples_here + jnp.arange(samples_here, dtype=jnp.int32)
    table = band_table(sample_times, band_bins, W)
    partial_value = jnp.einsum("wct,tk->wck", traces, table, preferred_element_type=F32)
    spectra_all = lax.psum(partial_value, "row")
    column_spectra = whiten(spectra_all, quality_mask)
    local_channels = traces.shape[1] // lax.axis_size("row")
    white = lax.dynamic_slice_in_dim(
        column_spectra, lax.axis_index("row") * local_channels, local_channels, 1
    )
    row_spectra = lax.all_gather(white, "col", axis=1, tiled=True)
    scale = 1.0 / math.sqrt(lax.axis_size("sub") * windows_here * nbins)
    partial_products = pair_products(row_spectra, column_spectra, band_bins, W)
    summed = lax.psum_scatter(partial_products, "sub", scatter_dimension=2, tiled=True)
    return summed * scale


def fill_table(first_sample, bins_ref, table_ref, coarse_ref, halfway):
    nbins = bins_ref.shape[1]
    runs = table_ref.shape[0] // FINE
    bins = bins_ref[...]

    def turn(ids, times):
        phase = (ids * times) & (W - 1)
        quarter = (phase + W // 8) // (W // 4)
        angle = (TWO_PI / W) * (phase - quarter * (W // 4)).astype(F32)
        square = angle * angle
        sine = jnp.full_like(square, 1.0 / 362880)
        for term in (-1.0 / 5040, 1.0 / 120, -1.0 / 6, 1.0):
            sine = sine * square + term
        sine = sine * angle
        cosine = jnp.full_like(square, -1.0 / 3628800)
        for term in (1.0 / 40320, -1.0 / 720, 1.0 / 24, -0.5, 1.0):
            cosine = cosine * square + term
        odd = (quarter & 1) == 1
        cosine, sine = jnp.where(odd, sine, cosine), jnp.where(odd, cosine, sine)
        cosine = jnp.where(((quarter + 1) & 2) == 2, -cosine, cosine)
        sine = jnp.where((quarter & 2) == 2, -sine, sine)
        return cosine, sine

    fine_times = lax.broadcasted_iota(jnp.int32, (FINE, nbins), 0)
    coarse_times = first_sample + FINE * lax.broadcasted_iota(jnp.int32, (runs, nbins), 0)
    cos_f, sin_f = turn(bins, fine_times)
    cos_h, sin_h = turn(1, fine_times)
    for place, value in enumerate(turn(bins, coarse_times) + turn(1, coarse_times)):
        coarse_ref[place] = value

    def fill(a):
        cos_c, sin_c, cos_g, sin_g = (coarse_ref[i, pl.ds(a, 1), :] for i in range(4))
        taper = 0.5 - 0.5 * (cos_g * cos_h - sin_g * sin_h)
        rows = pl.ds(pl.multiple_of(a * FINE, FINE), FINE)
        table_ref[rows, :nbins] = (taper * (cos_c * cos_f - sin_c * sin_f)).astype(BF16)
        table_ref[rows, nbins:] = (-taper * (sin_c * cos_f + cos_c * sin_f)).astype(BF16)

    pl.loop(0, runs // 2)(fill)
    halfway()
    pl.loop(runs // 2, runs)(fill)


def spectra_kernel(with_table, firsts, sizes, block, where_ref, bins_or_table, traces_ref, *rest):
    sides = len(sizes)
    outs, bufs, sems = rest[:sides], rest[-sides - 1 : -1], rest[-1]
    windows = traces_ref.shape[0]
    copies = []
    for w in range(windows):
        for i, size in enumerate(sizes):
            start = pl.multiple_of(where_ref[1 + i] * block + firsts[i], 128)
            copies.append(
                pltpu.make_async_copy(
                    traces_ref.at[w, pl.ds(start, size), :], bufs[i].at[w], sems.at[i, w]
                )
            )
    copies[0].start()
    if with_table:
        table_ref, coarse_ref = rest[sides : sides + 2]
        fill_table(where_ref[0], bins_or_table, table_ref, coarse_ref, copies[1].start)
    else:
        table_ref = bins_or_table
        copies[1].start()
    width = table_ref.shape[1]
    for index, copy in enumerate(copies):
        w, i = divmod(index, sides)
        copy.wait()
        if index + 2 < len(copies):
            copies[index + 2].start()
        outs[i][:, w * width : (w + 1) * width] = jnp.dot(
            bufs[i][w], table_ref[...], preferred_element_type=F32
        ).astype(outs[i].dtype)


def spectra_call(where, bins_or_table, traces, firsts, sizes, block, with_table, dtype):
    windows, _, samples = traces.shape
    nbins = bins_or_table.shape[1] if with_table else bins_or_table.shape[1] // 2
    lanes = windows * 2 * nbins
    vmem = pl.BlockSpec(memory_space=pltpu.VMEM)
    out_shape = [jax.ShapeDtypeStruct((size, lanes), dtype) for size in sizes]
    scratch = []
    if with_table:
        out_shape.append(jax.ShapeDtypeStruct((samples, 2 * nbins), BF16))
        scratch.append(pltpu.VMEM((4, samples // FINE, nbins), F32))
    scratch += [pltpu.VMEM((windows, size, samples), BF16) for size in sizes]
    scratch.append(pltpu.SemaphoreType.DMA((len(sizes), windows)))
    return pl.pallas_call(
        functools.partial(spectra_kernel, with_table, firsts, sizes, block),
        out_shape=out_shape,
        in_specs=[
            pl.BlockSpec(memory_space=pltpu.SMEM),
            vmem,
            pl.BlockSpec(memory_space=pl.ANY),
        ],
        out_specs=[vmem] * len(out_shape),
        scratch_shapes=scratch,
        compiler_params=pltpu.CompilerParams(vmem_limit_bytes=SPECTRA_VMEM),
        cost_estimate=SMALL,
        name="spectra",
    )(where, bins_or_table, traces)


def whiten_kernel(got, own, quality, white):
    nbins = got.shape[1] // 4
    mask = quality[...]
    for w in range(2):
        low = w * 2 * nbins
        high = low + nbins
        real = got[:, low : low + nbins].astype(F32) + own[:, low : low + nbins]
        imag = got[:, high : high + nbins].astype(F32) + own[:, high : high + nbins]
        power = real * real + imag * imag
        mean = jnp.sum(power, axis=1, keepdims=True) * (0.5 / nbins)
        factor = mask * jnp.minimum(lax.rsqrt(power), 4.0 * lax.rsqrt(mean + 1e-05))
        white[:, low : low + nbins] = (real * factor).astype(BF16)
        white[:, high : high + nbins] = (imag * factor).astype(BF16)


def whiten_call(got, own, quality):
    vmem = pl.BlockSpec(memory_space=pltpu.VMEM)
    return pl.pallas_call(
        whiten_kernel,
        out_shape=jax.ShapeDtypeStruct(got.shape, BF16),
        in_specs=[vmem] * 3,
        out_specs=vmem,
        compiler_params=pltpu.CompilerParams(vmem_limit_bytes=SMALL_VMEM),
        cost_estimate=SMALL,
        name="whiten",
    )(got, own, quality)


def place_tile(tiles, sems, out, index, sides, starts):
    block = tiles.shape[1]
    slot = index % tiles.shape[0]
    first = pl.multiple_of(sides[index // LAGS] * block, 128)
    return [
        pltpu.make_async_copy(
            tiles.at[slot, :, pl.ds(low, lanes)],
            out.at[index % LAGS, pl.ds(first, block), pl.ds(pl.multiple_of(start, 128), lanes)],
            sems.at[slot, i],
        )
        for i, (low, lanes, start) in enumerate(starts)
    ]


def times_columns(scale, rows, columns):
    return scale * lax.dot_general(
        rows, columns, (((1,), (1,)), ((), ())), preferred_element_type=F32
    )


def first_kernel(gather, scale, count, info, cos_ref, sin_ref, *refs):
    whites = refs[:4]
    parts = refs[4 : 4 + count]
    out, rows_out, columns, turned, tiles, sems, row_sems = refs[4 + count :]
    nbins = cos_ref.shape[1]
    half = whites[0].shape[1]
    gather(info, parts, columns)
    steps = 2 * LAGS

    def place(index):
        return place_tile(tiles, sems, out, index, info, [(0, tiles.shape[2], info[2])])[0]

    def keep(index):
        slot = lax.rem(index, 2)
        return pltpu.make_async_copy(turned.at[slot], rows_out.at[index], row_sems.at[slot])

    for side in range(2):

        @pl.loop(side * LAGS, (side + 1) * LAGS)
        def _(step):
            slot = lax.rem(step, 2)

            @pl.when(step >= 2)
            def _():
                place(step - 2).wait()
                keep(step - 2).wait()

            lag = lax.rem(step, LAGS)
            cosine = cos_ref[pl.ds(lag, 1), :]
            sine = sin_ref[pl.ds(lag, 1), :]
            for part in range(2):
                ref = whites[2 * side + part]
                for w in range(2):
                    low = w * 2 * nbins
                    high = low + nbins
                    real = ref[:, low : low + nbins].astype(F32)
                    imag = ref[:, high : high + nbins].astype(F32)
                    base = part * half
                    turned[slot, :, base + low : base + low + nbins] = (
                        real * cosine + imag * sine
                    ).astype(BF16)
                    turned[slot, :, base + high : base + high + nbins] = (
                        imag * cosine - real * sine
                    ).astype(BF16)
            keep(step).start()
            tiles[slot] = times_columns(scale, turned[slot], columns[...])
            place(step).start()

    for step in (steps - 2, steps - 1):
        place(step).wait()
        keep(step).wait()


def first_call(info, cosine, sine, whites, parts, gather, width, scale, out_shape):
    block, half = whites[0].shape
    vmem = pl.BlockSpec(memory_space=pltpu.VMEM)
    hbm = pl.BlockSpec(memory_space=pltpu.HBM)
    return pl.pallas_call(
        functools.partial(first_kernel, gather, scale, len(parts)),
        out_shape=[out_shape, jax.ShapeDtypeStruct((ROWS_KEPT, block, 2 * half), BF16)],
        in_specs=[pl.BlockSpec(memory_space=pltpu.SMEM)] + [vmem] * (6 + len(parts)),
        out_specs=[hbm, hbm],
        scratch_shapes=[
            pltpu.VMEM((width, 2 * half), BF16),
            pltpu.VMEM((2, block, 2 * half), BF16),
            pltpu.VMEM((2, block, width), F32),
            pltpu.SemaphoreType.DMA((2, 1)),
            pltpu.SemaphoreType.DMA((2,)),
        ],
        compiler_params=pltpu.CompilerParams(vmem_limit_bytes=PRODUCT_VMEM),
        cost_estimate=SMALL,
        name="turn_products",
    )(info, cosine, sine, *whites, *parts)


def product_kernel(gather, widths, scale, fetch, count, *refs):
    info, rows = refs[:2]
    parts = refs[2 : 2 + count]
    out = refs[3 + count]
    steps = 2 * LAGS
    if fetch:
        held, columns, tiles, sems, fetch_sems = refs[4 + count :]
    else:
        columns, tiles, sems = refs[4 + count :]
        held = rows

    lows = [sum(widths[:i]) for i in range(len(widths))]
    starts = [(lows[i], widths[i], info[2 + 2 * i]) for i in range(len(widths))]

    def start_placing(index):
        for copy in place_tile(tiles, sems, out, index, info, starts):
            copy.start()

    def end_placing(index):
        for copy in place_tile(tiles, sems, out, index, info, starts):
            copy.wait()

    def bring(index):
        return pltpu.make_async_copy(rows.at[index], held.at[index], fetch_sems.at[index])

    if fetch:
        for step in range(AHEAD):
            bring(step).start()
    gather(info, parts, columns)

    def run(step):
        if fetch:

            @pl.when(step + AHEAD < steps)
            def _():
                bring(step + AHEAD).start()

            bring(step).wait()

        @pl.when(step >= TILES)
        def _():
            end_placing(step - TILES)

        tiles[lax.rem(step, TILES)] = times_columns(scale, held[step], columns[...])
        start_placing(step)

    if fetch:
        pl.loop(0, steps)(run)
    else:
        for step in range(steps):
            if step >= TILES:
                end_placing(step - TILES)
            tiles[step % TILES] = times_columns(scale, held[step], columns[...])
            start_placing(step)
    for step in range(steps - TILES, steps):
        end_placing(step)


def product_call(info, rows, parts, gather, widths, scale, base, fetch):
    _, block, depth = rows.shape
    width = sum(widths)
    vmem = pl.BlockSpec(memory_space=pltpu.VMEM)
    hbm = pl.BlockSpec(memory_space=pltpu.HBM)
    out_shape = [jax.ShapeDtypeStruct(base.shape, base.dtype)]
    out_specs = [hbm]
    scratch = [
        pltpu.VMEM((width, depth), BF16),
        pltpu.VMEM((TILES, block, width), F32),
        pltpu.SemaphoreType.DMA((TILES, len(widths))),
    ]
    if fetch:
        out_shape.append(jax.ShapeDtypeStruct((2 * LAGS, block, depth), rows.dtype))
        out_specs.append(vmem)
        scratch.append(pltpu.SemaphoreType.DMA((2 * LAGS,)))
    return pl.pallas_call(
        functools.partial(product_kernel, gather, widths, scale, fetch, len(parts)),
        out_shape=out_shape,
        in_specs=[pl.BlockSpec(memory_space=pltpu.SMEM), hbm if fetch else vmem]
        + [vmem] * len(parts)
        + [hbm],
        out_specs=out_specs,
        scratch_shapes=scratch,
        input_output_aliases={2 + len(parts): 0},
        compiler_params=pltpu.CompilerParams(vmem_limit_bytes=PRODUCT_VMEM),
        cost_estimate=SMALL,
        name="products",
    )(info, rows, *parts, base)


def put(columns, first, rows, own, other):
    half = own.shape[1]
    count = rows.stop - rows.start
    columns[first : first + count, :half] = own[rows, :]
    columns[first : first + count, half:] = other[rows, :]


def gather_full(info, parts, columns):
    own_o, own_t, right_o, right_t, left_o, left_t = parts
    split, count = right_o.shape[0], columns.shape[0]

    @pl.when(info[3] == 1)
    def _():
        put(columns, 0, slice(0, count), own_o, own_t)

    @pl.when(info[3] == 0)
    def _():
        put(columns, 0, slice(0, split), right_o, right_t)
        put(columns, split, slice(0, count - split), left_o, left_t)


def gather_first(info, parts, columns):
    right_o, right_t, left_o, left_t = parts
    rows = slice(0, columns.shape[0])

    @pl.when(info[3] == 1)
    def _():
        put(columns, 0, rows, right_o, right_t)

    @pl.when(info[3] == 0)
    def _():
        put(columns, 0, rows, left_o, left_t)


def gather_last(info, parts, columns):
    early_o, early_t, right_o, right_t, left_o, left_t, own_o, own_t, tail_o, tail_t = parts
    split, rest = right_o.shape[0], left_o.shape[0]
    tail = columns.shape[0] - split

    @pl.when(info[3] == 1)
    def _():
        put(columns, 0, slice(rest, split), early_o, early_t)
        put(columns, split - rest, slice(0, rest), left_o, left_t)

    @pl.when(info[3] == 0)
    def _():
        put(columns, 0, slice(0, split), right_o, right_t)

    @pl.when(info[5] == 1)
    def _():
        put(columns, split, slice(own_o.shape[0] - tail, own_o.shape[0]), own_o, own_t)

    @pl.when(info[5] == 0)
    def _():
        put(columns, split, slice(tail_o.shape[0] - tail, tail_o.shape[0]), tail_o, tail_t)


def local_rings(traces, quality_mask, band_bins):
    n = lax.axis_size("row")
    windows, channels, samples = traces.shape
    nbins = band_bins.shape[0]
    block = channels // n
    split = (block // 128 + 1) // 2 * 128
    rest = block - split
    z = lax.axis_index("row")
    x = lax.axis_index("col")
    c = lax.axis_index("sub")
    to_right = [(i, (i + 1) % n) for i in range(n)]
    to_left = [(i, (i - 1) % n) for i in range(n)]
    i32 = jnp.int32

    def where(*blocks):
        return jnp.stack([z * samples, *(b % n for b in blocks)]).astype(i32)

    right, left, table = spectra_call(
        where(z - 1, z + 1), band_bins[None, :], traces, (0, split), (split, rest), block, True, BF16
    )
    for k in range(1, n):
        places = where(z - 1 - k, z + 1 + k)
        if k > 1:
            places = lax.optimization_barrier((places, right, left))[0]
        own_r, own_l = spectra_call(
            places, table, traces, (0, split), (split, rest), block, False, F32
        )
        right = lax.ppermute(right, "row", to_right)
        left = lax.ppermute(left, "row", to_left)
        if k < n - 1:
            right = (right.astype(F32) + own_r).astype(BF16)
            left = (left.astype(F32) + own_l).astype(BF16)
    quality = lax.dynamic_slice_in_dim(quality_mask, z * block, block).astype(F32)[:, None]
    right = whiten_call(right, own_r, quality[:split])
    left = whiten_call(left, own_l, quality[split:])
    white = jnp.concatenate([right, left], axis=0)

    def pairs(step, move, cross):
        found = []
        for i in range(n):
            core = (i - step * move) % n * 2 // n
            source = 1 - core if cross else core
            found.append((i * 2 + source, (i + move) % n * 2 + core))
        return found

    def last_step(part, move):
        return [lax.ppermute(part, axes, pairs(n - 2, move, cross)) for cross in (False, True)]

    axes = ("row", "sub")
    swap = [(0, 1), (1, 0)]
    right0 = lax.ppermute(right, "row", to_right)
    left0 = lax.ppermute(left, "row", to_left)
    white_t = lax.ppermute(white, "sub", swap)
    far = lax.ppermute(white, "col", swap)
    right1 = lax.ppermute(right0, "row", to_right)
    left1 = lax.ppermute(left0, "row", to_left)
    r0 = [right0, lax.ppermute(right0, "sub", swap)]
    l0 = [left0, lax.ppermute(left0, "sub", swap)]
    far_t = lax.ppermute(far, "sub", swap)

    shifts = jnp.array([(lag - LAGS // 2) * LAG_STEP for lag in range(LAGS)], i32)
    angles = TWO_PI / W * (band_bins[None, :] * shifts[:, None] % W).astype(F32)
    cosine, sine = jnp.cos(angles), jnp.sin(angles)
    tail = 128
    per_core = n // 2
    owner = z // per_core == c
    from_right = (z - 1) % n // per_core == c
    full = jnp.where(owner, z, (z + 2) % n) - per_core * c
    other = 1 - full
    scale = 1.0 / math.sqrt(2 * windows * nbins)
    out_shape = jax.ShapeDtypeStruct((LAGS, 2 * block, per_core * block), F32)
    first_start = other * block + jnp.where(from_right, 0, split)
    last_start = other * block + jnp.where(from_right, rest, 0)

    def info(*places):
        return jnp.stack([x, 1 - x, *places]).astype(i32)

    result, rows = first_call(
        info(first_start, from_right), cosine, sine, [white, white_t, far, far_t], r0 + l0,
        gather_first, rest, scale, out_shape,
    )
    right1 = lax.optimization_barrier((right1, result))[0]
    left1 = lax.optimization_barrier((left1, result))[0]
    r2 = last_step(right1, 1)
    l2 = last_step(left1, -1)
    r1 = [right1, lax.ppermute(right1, "sub", swap)]
    l1 = [left1, lax.ppermute(left1, "sub", swap)]
    result, rows = product_call(
        info(full * block, owner), rows, [white, white_t] + r1 + l1,
        gather_full, (block - tail,), scale, result, True,
    )
    return product_call(
        info(last_start, from_right, full * block + block - tail, owner), rows,
        r0 + r2 + l2 + [white, white_t] + l1, gather_last, (split, tail), scale, result, False,
    )[0]


def solution(mesh):
    in_specs = (P(("group", "sub"), "col", "row"), P("col"), P())
    out_specs = P("group", "row", ("col", "sub"))
    rings = (mesh.shape["row"], mesh.shape["col"], mesh.shape["sub"]) == (4, 2, 2)
    return jax.shard_map(
        local_rings if rings else local_plain,
        mesh=mesh, in_specs=in_specs, out_specs=out_specs, check_vma=False,
    )
```

```python
import functools
import math

import jax
import jax.numpy as jnp
from jax import lax
from jax.experimental import pallas as pl
from jax.experimental.pallas import tpu as pltpu
from jax.sharding import PartitionSpec as P

W = 16384
LAGS = 4
LAG_STEP = 50
TWO_PI = 2.0 * math.pi

F32 = jnp.float32
BF16 = jnp.bfloat16
MIB = 1024 * 1024
SPECTRA_VMEM = 18 * MIB
SMALL_VMEM = 8 * MIB
PRODUCT_VMEM = 20 * MIB
SMALL = pl.CostEstimate(flops=1000, bytes_accessed=1000, transcendentals=0)
TILES = 4
AHEAD = 5
ROWS_KEPT = 48
FINE = 64


def band_table(sample_times, bin_ids, length):
    window_taper = 0.5 - 0.5 * jnp.cos(TWO_PI / length * sample_times.astype(F32))
    phase_index = sample_times[:, None] * bin_ids[None, :] % length
    angles = TWO_PI / length * phase_index.astype(F32)
    cosine = window_taper[:, None] * jnp.cos(angles)
    sine_part = -window_taper[:, None] * jnp.sin(angles)
    return jnp.concatenate([cosine, sine_part], axis=1).astype(BF16)


def whiten(spectra, quality):
    nbins = spectra.shape[-1] // 2
    real_part = spectra[..., :nbins]
    imag_part = spectra[..., nbins:]
    band_rms = jnp.sqrt(jnp.mean(spectra * spectra, axis=-1, keepdims=True) + 1e-05)
    magnitude = jnp.sqrt(real_part * real_part + imag_part * imag_part)
    divisor = jnp.maximum(magnitude, 0.25 * band_rms)
    scaled = jnp.concatenate([real_part / divisor, imag_part / divisor], axis=-1)
    return (quality.astype(F32)[:, None] * scaled).astype(BF16)


def rotate(white, bin_ids, lag_shift, length):
    nbins = white.shape[-1] // 2
    phase_index = bin_ids * lag_shift % length
    angles = TWO_PI / length * phase_index.astype(F32)
    cosine = jnp.cos(angles)
    sine_part = jnp.sin(angles)
    real_part = white[..., :nbins].astype(F32)
    imag_part = white[..., nbins:].astype(F32)
    turned = jnp.concatenate(
        [real_part * cosine + imag_part * sine_part, imag_part * cosine - real_part * sine_part],
        axis=-1,
    )
    return turned.astype(BF16)


def pair_products(row_spectra, column_spectra, bin_ids, length):
    results = []
    for lag_index in range(LAGS):
        lag_shift = (lag_index - LAGS // 2) * LAG_STEP
        rotated = rotate(row_spectra, bin_ids, lag_shift, length)
        results.append(
            jnp.einsum("wpk,wqk->pq", rotated, column_spectra, preferred_element_type=F32)
        )
    return jnp.stack(results)


def local_plain(traces, quality_mask, band_bins):
    nbins = band_bins.shape[0]
    windows_here = traces.shape[0]
    samples_here = traces.shape[2]
    sample_times = lax.axis_index("row") * samples_here + jnp.arange(samples_here, dtype=jnp.int32)
    table = band_table(sample_times, band_bins, W)
    partial_value = jnp.einsum("wct,tk->wck", traces, table, preferred_element_type=F32)
    spectra_all = lax.psum(partial_value, "row")
    column_spectra = whiten(spectra_all, quality_mask)
    local_channels = traces.shape[1] // lax.axis_size("row")
    white = lax.dynamic_slice_in_dim(
        column_spectra, lax.axis_index("row") * local_channels, local_channels, 1
    )
    row_spectra = lax.all_gather(white, "col", axis=1, tiled=True)
    scale = 1.0 / math.sqrt(lax.axis_size("sub") * windows_here * nbins)
    partial_products = pair_products(row_spectra, column_spectra, band_bins, W)
    summed = lax.psum_scatter(partial_products, "sub", scatter_dimension=2, tiled=True)
    return summed * scale


def fill_table(first_sample, bins_ref, table_ref, coarse_ref, halfway):
    nbins = bins_ref.shape[1]
    runs = table_ref.shape[0] // FINE
    bins = bins_ref[...]

    def turn(ids, times):
        phase = (ids * times) & (W - 1)
        quarter = (phase + W // 8) // (W // 4)
        angle = (TWO_PI / W) * (phase - quarter * (W // 4)).astype(F32)
        square = angle * angle
        sine = jnp.full_like(square, 1.0 / 362880)
        for term in (-1.0 / 5040, 1.0 / 120, -1.0 / 6, 1.0):
            sine = sine * square + term
        sine = sine * angle
        cosine = jnp.full_like(square, -1.0 / 3628800)
        for term in (1.0 / 40320, -1.0 / 720, 1.0 / 24, -0.5, 1.0):
            cosine = cosine * square + term
        odd = (quarter & 1) == 1
        cosine, sine = jnp.where(odd, sine, cosine), jnp.where(odd, cosine, sine)
        cosine = jnp.where(((quarter + 1) & 2) == 2, -cosine, cosine)
        sine = jnp.where((quarter & 2) == 2, -sine, sine)
        return cosine, sine

    fine_times = lax.broadcasted_iota(jnp.int32, (FINE, nbins), 0)
    coarse_times = first_sample + FINE * lax.broadcasted_iota(jnp.int32, (runs, nbins), 0)
    cos_f, sin_f = turn(bins, fine_times)
    cos_h, sin_h = turn(1, fine_times)
    for place, value in enumerate(turn(bins, coarse_times) + turn(1, coarse_times)):
        coarse_ref[place] = value

    def fill(a):
        cos_c, sin_c, cos_g, sin_g = (coarse_ref[i, pl.ds(a, 1), :] for i in range(4))
        taper = 0.5 - 0.5 * (cos_g * cos_h - sin_g * sin_h)
        rows = pl.ds(pl.multiple_of(a * FINE, FINE), FINE)
        table_ref[rows, :nbins] = (taper * (cos_c * cos_f - sin_c * sin_f)).astype(BF16)
        table_ref[rows, nbins:] = (-taper * (sin_c * cos_f + cos_c * sin_f)).astype(BF16)

    pl.loop(0, runs // 2)(fill)
    halfway()
    pl.loop(runs // 2, runs)(fill)


def spectra_kernel(with_table, firsts, sizes, block, where_ref, bins_or_table, traces_ref, *rest):
    sides = len(sizes)
    outs, bufs, sems = rest[:sides], rest[-sides - 1 : -1], rest[-1]
    windows = traces_ref.shape[0]
    copies = []
    for w in range(windows):
        for i, size in enumerate(sizes):
            start = pl.multiple_of(where_ref[1 + i] * block + firsts[i], 128)
            copies.append(
                pltpu.make_async_copy(
                    traces_ref.at[w, pl.ds(start, size), :], bufs[i].at[w], sems.at[i, w]
                )
            )
    copies[0].start()
    if with_table:
        table_ref, coarse_ref = rest[sides : sides + 2]
        fill_table(where_ref[0], bins_or_table, table_ref, coarse_ref, copies[1].start)
    else:
        table_ref = bins_or_table
        copies[1].start()
    width = table_ref.shape[1]
    for index, copy in enumerate(copies):
        w, i = divmod(index, sides)
        copy.wait()
        if index + 2 < len(copies):
            copies[index + 2].start()
        outs[i][:, w * width : (w + 1) * width] = jnp.dot(
            bufs[i][w], table_ref[...], preferred_element_type=F32
        ).astype(outs[i].dtype)


def spectra_call(where, bins_or_table, traces, firsts, sizes, block, with_table, dtype):
    windows, _, samples = traces.shape
    nbins = bins_or_table.shape[1] if with_table else bins_or_table.shape[1] // 2
    lanes = windows * 2 * nbins
    vmem = pl.BlockSpec(memory_space=pltpu.VMEM)
    out_shape = [jax.ShapeDtypeStruct((size, lanes), dtype) for size in sizes]
    scratch = []
    if with_table:
        out_shape.append(jax.ShapeDtypeStruct((samples, 2 * nbins), BF16))
        scratch.append(pltpu.VMEM((4, samples // FINE, nbins), F32))
    scratch += [pltpu.VMEM((windows, size, samples), BF16) for size in sizes]
    scratch.append(pltpu.SemaphoreType.DMA((len(sizes), windows)))
    return pl.pallas_call(
        functools.partial(spectra_kernel, with_table, firsts, sizes, block),
        out_shape=out_shape,
        in_specs=[
            pl.BlockSpec(memory_space=pltpu.SMEM),
            vmem,
            pl.BlockSpec(memory_space=pl.ANY),
        ],
        out_specs=[vmem] * len(out_shape),
        scratch_shapes=scratch,
        compiler_params=pltpu.CompilerParams(vmem_limit_bytes=SPECTRA_VMEM),
        cost_estimate=SMALL,
        name="spectra",
    )(where, bins_or_table, traces)


def whiten_kernel(got, own, quality, white):
    nbins = got.shape[1] // 4
    mask = quality[...]
    for w in range(2):
        low = w * 2 * nbins
        high = low + nbins
        real = got[:, low : low + nbins].astype(F32) + own[:, low : low + nbins]
        imag = got[:, high : high + nbins].astype(F32) + own[:, high : high + nbins]
        power = real * real + imag * imag
        mean = jnp.sum(power, axis=1, keepdims=True) * (0.5 / nbins)
        factor = mask * jnp.minimum(lax.rsqrt(power), 4.0 * lax.rsqrt(mean + 1e-05))
        white[:, low : low + nbins] = (real * factor).astype(BF16)
        white[:, high : high + nbins] = (imag * factor).astype(BF16)


def whiten_call(got, own, quality):
    vmem = pl.BlockSpec(memory_space=pltpu.VMEM)
    return pl.pallas_call(
        whiten_kernel,
        out_shape=jax.ShapeDtypeStruct(got.shape, BF16),
        in_specs=[vmem] * 3,
        out_specs=vmem,
        compiler_params=pltpu.CompilerParams(vmem_limit_bytes=SMALL_VMEM),
        cost_estimate=SMALL,
        name="whiten",
    )(got, own, quality)


def place_tile(tiles, sems, out, index, sides, starts):
    block = tiles.shape[1]
    slot = index % tiles.shape[0]
    first = pl.multiple_of(sides[index // LAGS] * block, 128)
    return [
        pltpu.make_async_copy(
            tiles.at[slot, :, pl.ds(low, lanes)],
            out.at[index % LAGS, pl.ds(first, block), pl.ds(pl.multiple_of(start, 128), lanes)],
            sems.at[slot, i],
        )
        for i, (low, lanes, start) in enumerate(starts)
    ]


def times_columns(scale, rows, columns):
    return scale * lax.dot_general(
        rows, columns, (((1,), (1,)), ((), ())), preferred_element_type=F32
    )


def first_kernel(gather, scale, count, info, cos_ref, sin_ref, *refs):
    whites = refs[:4]
    parts = refs[4 : 4 + count]
    out, rows_out, columns, turned, tiles, sems, row_sems = refs[4 + count :]
    nbins = cos_ref.shape[1]
    half = whites[0].shape[1]
    gather(info, parts, columns)
    steps = 2 * LAGS

    def place(index):
        return place_tile(tiles, sems, out, index, info, [(0, tiles.shape[2], info[2])])[0]

    def keep(index):
        slot = lax.rem(index, 2)
        return pltpu.make_async_copy(turned.at[slot], rows_out.at[index], row_sems.at[slot])

    for side in range(2):

        @pl.loop(side * LAGS, (side + 1) * LAGS)
        def _(step):
            slot = lax.rem(step, 2)

            @pl.when(step >= 2)
            def _():
                place(step - 2).wait()
                keep(step - 2).wait()

            lag = lax.rem(step, LAGS)
            cosine = cos_ref[pl.ds(lag, 1), :]
            sine = sin_ref[pl.ds(lag, 1), :]
            for part in range(2):
                ref = whites[2 * side + part]
                for w in range(2):
                    low = w * 2 * nbins
                    high = low + nbins
                    real = ref[:, low : low + nbins].astype(F32)
                    imag = ref[:, high : high + nbins].astype(F32)
                    base = part * half
                    turned[slot, :, base + low : base + low + nbins] = (
                        real * cosine + imag * sine
                    ).astype(BF16)
                    turned[slot, :, base + high : base + high + nbins] = (
                        imag * cosine - real * sine
                    ).astype(BF16)
            keep(step).start()
            tiles[slot] = times_columns(scale, turned[slot], columns[...])
            place(step).start()

    for step in (steps - 2, steps - 1):
        place(step).wait()
        keep(step).wait()


def first_call(info, cosine, sine, whites, parts, gather, width, scale, out_shape):
    block, half = whites[0].shape
    vmem = pl.BlockSpec(memory_space=pltpu.VMEM)
    hbm = pl.BlockSpec(memory_space=pltpu.HBM)
    return pl.pallas_call(
        functools.partial(first_kernel, gather, scale, len(parts)),
        out_shape=[out_shape, jax.ShapeDtypeStruct((ROWS_KEPT, block, 2 * half), BF16)],
        in_specs=[pl.BlockSpec(memory_space=pltpu.SMEM)] + [vmem] * (6 + len(parts)),
        out_specs=[hbm, hbm],
        scratch_shapes=[
            pltpu.VMEM((width, 2 * half), BF16),
            pltpu.VMEM((2, block, 2 * half), BF16),
            pltpu.VMEM((2, block, width), F32),
            pltpu.SemaphoreType.DMA((2, 1)),
            pltpu.SemaphoreType.DMA((2,)),
        ],
        compiler_params=pltpu.CompilerParams(vmem_limit_bytes=PRODUCT_VMEM),
        cost_estimate=SMALL,
        name="turn_products",
    )(info, cosine, sine, *whites, *parts)


def product_kernel(gather, widths, scale, fetch, count, *refs):
    info, rows = refs[:2]
    parts = refs[2 : 2 + count]
    out = refs[3 + count]
    steps = 2 * LAGS
    if fetch:
        held, columns, tiles, sems, fetch_sems = refs[4 + count :]
    else:
        columns, tiles, sems = refs[4 + count :]
        held = rows

    lows = [sum(widths[:i]) for i in range(len(widths))]
    starts = [(lows[i], widths[i], info[2 + 2 * i]) for i in range(len(widths))]

    def start_placing(index):
        for copy in place_tile(tiles, sems, out, index, info, starts):
            copy.start()

    def end_placing(index):
        for copy in place_tile(tiles, sems, out, index, info, starts):
            copy.wait()

    def bring(index):
        return pltpu.make_async_copy(rows.at[index], held.at[index], fetch_sems.at[index])

    if fetch:
        for step in range(AHEAD):
            bring(step).start()
    gather(info, parts, columns)

    def run(step):
        if fetch:

            @pl.when(step + AHEAD < steps)
            def _():
                bring(step + AHEAD).start()

            bring(step).wait()

        @pl.when(step >= TILES)
        def _():
            end_placing(step - TILES)

        tiles[lax.rem(step, TILES)] = times_columns(scale, held[step], columns[...])
        start_placing(step)

    if fetch:
        pl.loop(0, steps)(run)
    else:
        for step in range(steps):
            if step >= TILES:
                end_placing(step - TILES)
            tiles[step % TILES] = times_columns(scale, held[step], columns[...])
            start_placing(step)
    for step in range(steps - TILES, steps):
        end_placing(step)


def product_call(info, rows, parts, gather, widths, scale, base, fetch):
    _, block, depth = rows.shape
    width = sum(widths)
    vmem = pl.BlockSpec(memory_space=pltpu.VMEM)
    hbm = pl.BlockSpec(memory_space=pltpu.HBM)
    out_shape = [jax.ShapeDtypeStruct(base.shape, base.dtype)]
    out_specs = [hbm]
    scratch = [
        pltpu.VMEM((width, depth), BF16),
        pltpu.VMEM((TILES, block, width), F32),
        pltpu.SemaphoreType.DMA((TILES, len(widths))),
    ]
    if fetch:
        out_shape.append(jax.ShapeDtypeStruct((2 * LAGS, block, depth), rows.dtype))
        out_specs.append(vmem)
        scratch.append(pltpu.SemaphoreType.DMA((2 * LAGS,)))
    return pl.pallas_call(
        functools.partial(product_kernel, gather, widths, scale, fetch, len(parts)),
        out_shape=out_shape,
        in_specs=[pl.BlockSpec(memory_space=pltpu.SMEM), hbm if fetch else vmem]
        + [vmem] * len(parts)
        + [hbm],
        out_specs=out_specs,
        scratch_shapes=scratch,
        input_output_aliases={2 + len(parts): 0},
        compiler_params=pltpu.CompilerParams(vmem_limit_bytes=PRODUCT_VMEM),
        cost_estimate=SMALL,
        name="products",
    )(info, rows, *parts, base)


def put(columns, first, rows, own, other):
    half = own.shape[1]
    count = rows.stop - rows.start
    columns[first : first + count, :half] = own[rows, :]
    columns[first : first + count, half:] = other[rows, :]


def gather_full(info, parts, columns):
    own_o, own_t, right_o, right_t, left_o, left_t = parts
    split, count = right_o.shape[0], columns.shape[0]

    @pl.when(info[3] == 1)
    def _():
        put(columns, 0, slice(0, count), own_o, own_t)

    @pl.when(info[3] == 0)
    def _():
        put(columns, 0, slice(0, split), right_o, right_t)
        put(columns, split, slice(0, count - split), left_o, left_t)


def gather_first(info, parts, columns):
    right_o, right_t, left_o, left_t = parts
    rows = slice(0, columns.shape[0])

    @pl.when(info[3] == 1)
    def _():
        put(columns, 0, rows, right_o, right_t)

    @pl.when(info[3] == 0)
    def _():
        put(columns, 0, rows, left_o, left_t)


def gather_last(info, parts, columns):
    early_o, early_t, right_o, right_t, left_o, left_t, own_o, own_t, tail_o, tail_t = parts
    split, rest = right_o.shape[0], left_o.shape[0]
    tail = columns.shape[0] - split

    @pl.when(info[3] == 1)
    def _():
        put(columns, 0, slice(rest, split), early_o, early_t)
        put(columns, split - rest, slice(0, rest), left_o, left_t)

    @pl.when(info[3] == 0)
    def _():
        put(columns, 0, slice(0, split), right_o, right_t)

    @pl.when(info[5] == 1)
    def _():
        put(columns, split, slice(own_o.shape[0] - tail, own_o.shape[0]), own_o, own_t)

    @pl.when(info[5] == 0)
    def _():
        put(columns, split, slice(tail_o.shape[0] - tail, tail_o.shape[0]), tail_o, tail_t)


def local_rings(traces, quality_mask, band_bins):
    n = lax.axis_size("row")
    windows, channels, samples = traces.shape
    nbins = band_bins.shape[0]
    block = channels // n
    split = (block // 128 + 1) // 2 * 128
    rest = block - split
    z = lax.axis_index("row")
    x = lax.axis_index("col")
    c = lax.axis_index("sub")
    to_right = [(i, (i + 1) % n) for i in range(n)]
    to_left = [(i, (i - 1) % n) for i in range(n)]
    i32 = jnp.int32

    def where(*blocks):
        return jnp.stack([z * samples, *(b % n for b in blocks)]).astype(i32)

    right, left, table = spectra_call(
        where(z - 1, z + 1), band_bins[None, :], traces, (0, split), (split, rest), block, True, BF16
    )
    for k in range(1, n):
        places = where(z - 1 - k, z + 1 + k)
        if k > 1:
            places = lax.optimization_barrier((places, right, left))[0]
        own_r, own_l = spectra_call(
            places, table, traces, (0, split), (split, rest), block, False, F32
        )
        right = lax.ppermute(right, "row", to_right)
        left = lax.ppermute(left, "row", to_left)
        if k < n - 1:
            right = (right.astype(F32) + own_r).astype(BF16)
            left = (left.astype(F32) + own_l).astype(BF16)
    quality = lax.dynamic_slice_in_dim(quality_mask, z * block, block).astype(F32)[:, None]
    right = whiten_call(right, own_r, quality[:split])
    left = whiten_call(left, own_l, quality[split:])
    white = jnp.concatenate([right, left], axis=0)

    def pairs(step, move, cross):
        found = []
        for i in range(n):
            core = (i - step * move) % n * 2 // n
            source = 1 - core if cross else core
            found.append((i * 2 + source, (i + move) % n * 2 + core))
        return found

    def last_step(part, move):
        return [lax.ppermute(part, axes, pairs(n - 2, move, cross)) for cross in (False, True)]

    axes = ("row", "sub")
    swap = [(0, 1), (1, 0)]
    right0 = lax.ppermute(right, "row", to_right)
    left0 = lax.ppermute(left, "row", to_left)
    white_t = lax.ppermute(white, "sub", swap)
    far = lax.ppermute(white, "col", swap)
    right1 = lax.ppermute(right0, "row", to_right)
    left1 = lax.ppermute(left0, "row", to_left)
    r0 = [right0, lax.ppermute(right0, "sub", swap)]
    l0 = [left0, lax.ppermute(left0, "sub", swap)]
    far_t = lax.ppermute(far, "sub", swap)

    shifts = jnp.array([(lag - LAGS // 2) * LAG_STEP for lag in range(LAGS)], i32)
    angles = TWO_PI / W * (band_bins[None, :] * shifts[:, None] % W).astype(F32)
    cosine, sine = jnp.cos(angles), jnp.sin(angles)
    tail = 128
    per_core = n // 2
    owner = z // per_core == c
    from_right = (z - 1) % n // per_core == c
    full = jnp.where(owner, z, (z + 2) % n) - per_core * c
    other = 1 - full
    scale = 1.0 / math.sqrt(2 * windows * nbins)
    out_shape = jax.ShapeDtypeStruct((LAGS, 2 * block, per_core * block), F32)
    first_start = other * block + jnp.where(from_right, 0, split)
    last_start = other * block + jnp.where(from_right, rest, 0)

    def info(*places):
        return jnp.stack([x, 1 - x, *places]).astype(i32)

    result, rows = first_call(
        info(first_start, from_right), cosine, sine, [white, white_t, far, far_t], r0 + l0,
        gather_first, rest, scale, out_shape,
    )
    right1 = lax.optimization_barrier((right1, result))[0]
    left1 = lax.optimization_barrier((left1, result))[0]
    r2 = last_step(right1, 1)
    l2 = last_step(left1, -1)
    r1 = [right1, lax.ppermute(right1, "sub", swap)]
    l1 = [left1, lax.ppermute(left1, "sub", swap)]
    result, rows = product_call(
        info(full * block, owner), rows, [white, white_t] + r1 + l1,
        gather_full, (block - tail,), scale, result, True,
    )
    return product_call(
        info(last_start, from_right, full * block + block - tail, owner), rows,
        r0 + r2 + l2 + [white, white_t] + l1, gather_last, (split, tail), scale, result, False,
    )[0]


def solution(mesh):
    in_specs = (P(("group", "sub"), "col", "row"), P("col"), P())
    out_specs = P("group", "row", ("col", "sub"))
    rings = (mesh.shape["row"], mesh.shape["col"], mesh.shape["sub"]) == (4, 2, 2)
    return jax.shard_map(
        local_rings if rings else local_plain,
        mesh=mesh, in_specs=in_specs, out_specs=out_specs, check_vma=False,
    )
```
